256 devices in a mesh: group: 4 (over x), shard: 64 (over z, y, core).
Axes of the slice: x: 4, y: 4, z: 8, core: 2. Of those that a mesh axis runs over, the one named last changes fastest.
Arguments:
- delta: float32 [4, 3072, 5120], P('group', 'shard'), as said below
- error: float32 [4, 3072, 5120], P('group', 'shard'), may hold values from -4 to 4
- weights: float32 [3072, 5120], P('shard'), may hold values from -0.75 to 0.75
- momentum: float32 [3072, 5120], P('shard'), may hold values from -3 to 3
- anchor: float32 [3072, 5120], P('shard'), may hold values from -0.75 to 0.75
- basis: float32 [5120, 64], replicated, may hold values from -0.078125 to 0.078125
Outputs:
- new_weights: float32 [3072, 5120], P('shard')
- new_momentum: float32 [3072, 5120], P('shard')
- new_anchor: float32 [3072, 5120], P('shard')
- new_error: float32 [4, 3072, 5120], P('group', 'shard')
- new_basis: float32 [5120, 64], replicated
The draws below stay inside these ranges and needn't reach their ends.
Inputs may be any that keep to these rules, and one draw needn't show every extreme that they name: `delta`: Real-valued pseudo-gradients of full rank.
All inputs are finite; a program needn't handle non-finite values.
Results may differ from the reference program's by a relative error of at most 0.00027.
Values sent between devices are 32-bit elements; how exact they have to be, the bound alone decides.
A program may use at most 64 MiB of HBM per device.

```python
import jax
import jax.numpy as jnp
from jax import lax

D = 5120
RANK = 64
ROWS = 3072
N_GROUP = 4


def draw_delta(key, part):
    key = jax.random.fold_in(key, 11)
    key_own, key_cols = jax.random.split(key, 2)
    position = jnp.arange(ROWS, dtype=jnp.float32) / (ROWS - 1)
    columns = jnp.exp(jax.random.uniform(key_cols, (D,), minval=-0.7, maxval=0.7))
    ramp = 10.0 ** (position - 0.5)
    base = jax.random.normal(key_own, (N_GROUP, ROWS, D))
    return (base * ramp[None, :, None] * columns[None, None, :]).astype(jnp.float32)


def block_levels(key, shape, cuts, least, high):
    level, own = 1.0, jax.random.fold_in(key, 6)
    for axis_at, parts in cuts:
        heights = jnp.exp(jax.random.uniform(jax.random.fold_in(own, axis_at), (parts,), jnp.float32, least / len(cuts), high / len(cuts)))
        level = level * jnp.repeat(heights, shape[axis_at] // parts).reshape([-1 if axis == axis_at else 1 for axis in range(len(shape))])
    return level


def noise(rng, shape, width, bound, shards=(), held_as=jnp.bfloat16):
    level = block_levels(rng, shape, shards, -0.22, 0.18) if shards else 1.0
    result = jax.random.normal(rng, shape, jnp.float32) * width * level
    return jnp.minimum(jnp.maximum(result, -bound), bound).astype(held_as)


def setup_inputs(seed: int = 0) -> dict:
    keys = jax.random.split(jax.random.key(seed), 7)
    delta = draw_delta(jax.random.fold_in(keys[6], 71), 0)
    error = noise(keys[1], (N_GROUP, ROWS, D), 0.3, 4.0, ((0, 4), (1, 64)), jnp.float32)
    weights = noise(keys[2], (ROWS, D), 0.05, 0.75, ((0, 64),), jnp.float32)
    momentum = noise(keys[3], (ROWS, D), 0.2, 3.0, ((0, 64),), jnp.float32)
    anchor = noise(keys[4], (ROWS, D), 0.05, 0.75, ((0, 64),), jnp.float32)
    basis = noise(keys[5], (D, RANK), D ** -0.5, 0.078125, (), jnp.float32)
    return dict(delta=delta, error=error, weights=weights, momentum=momentum, anchor=anchor, basis=basis)


outer_rate = 0.7
nesterov_mu = 0.9
anchor_decay = 0.9

def reference(delta, error, weights, momentum, anchor, basis):
    highest = lax.Precision.HIGHEST
    merged = delta + error
    left = jnp.zeros((ROWS, RANK), jnp.float32)
    for index in range(N_GROUP):
        left = left + jnp.dot(merged[index].astype(jnp.float32), basis.astype(jnp.float32), precision=highest, preferred_element_type=jnp.float32)
    gram = jnp.dot(left.T.astype(jnp.float32), left.astype(jnp.float32), precision=highest, preferred_element_type=jnp.float32)
    chol = jnp.linalg.cholesky(gram)
    ortho = jax.scipy.linalg.solve_triangular(chol, left.T, lower=True).T
    right = jnp.zeros((D, RANK), jnp.float32)
    for index in range(N_GROUP):
        right = right + jnp.dot(merged[index].T.astype(jnp.float32), ortho.astype(jnp.float32), precision=highest, preferred_element_type=jnp.float32)
    new_basis = right / N_GROUP
    approx = jnp.dot(ortho.astype(jnp.float32), new_basis.T.astype(jnp.float32), precision=highest, preferred_element_type=jnp.float32)
    new_error = merged - approx[None]
    new_momentum = nesterov_mu * momentum + approx
    new_weights = weights - outer_rate * (approx + nesterov_mu * new_momentum)
    new_anchor = anchor_decay * anchor + (1.0 - anchor_decay) * new_weights
    return (new_weights, new_momentum, new_anchor, new_error, new_basis)
```

```python
import jax
import jax.numpy as jnp
from jax import lax
from jax.experimental import pallas as pl
from jax.experimental.pallas import tpu as pltpu
from jax.sharding import PartitionSpec as P

MESH = pl.DeviceIdType.MESH
HIGHEST = lax.Precision.HIGHEST
F32 = jnp.float32

outer_rate = 0.7
nesterov_mu = 0.9
anchor_decay = 0.9

D = 5120
RANK = 64
ROWS = 48
NX, NY, NZ = 4, 4, 8
HALF = D // 2
QUARTER = HALF // 4
CHUNKS = ((0, 384), (384, 256))
LOAD = 1280
ZORDER = (4, 3, 5, 2, 6, 1, 7)


def hint(value, multiple):
    return pl.multiple_of(value, multiple)


def dot_nt(a, b):
    return lax.dot_general(a, b, (((1,), (1,)), ((), ())), precision=HIGHEST, preferred_element_type=F32)


def dot_tn(a, b):
    return lax.dot_general(a, b, (((0,), (0,)), ((), ())), precision=HIGHEST, preferred_element_type=F32)


def dot(a, b):
    return jnp.dot(a, b, precision=HIGHEST, preferred_element_type=F32)


def eliminate(aug, first, last):
    for j in range(first, last):
        block = j // 8 * 8
        pivot = aug[j : j + 1, j : j + 1]
        scale = lax.rsqrt(pivot)
        scale = scale * (1.5 - 0.5 * pivot * scale * scale)
        row = aug[j : j + 1, :] * scale
        tail = aug[block:, :]
        index = lax.broadcasted_iota(jnp.int32, tail.shape, 0) + block
        moved = tail - (tail[:, j : j + 1] * scale) * row
        tail = jnp.where(index > j, moved, jnp.where(index == j, row, tail))
        aug[block:, :] = tail


def reduce_kernel(
    delta, error, basis_t, merged, total, coef,
    d_buf, e_buf, b_buf, mcat, lbuf, l96, tsend, p1, s1, p2, p3, gfull, gy, gz, gsum, aug,
    load_sem, sib_sem, left_sem, p1_sem, p2_sem, p3_sem, p4_sem, p5_sem, fwd_sem, gy_sem, gz_sem, gs_sem,
):
    x = lax.axis_index("group")
    shard = lax.axis_index("shard")
    z = shard // 8
    y = (shard // 2) % 4
    c = shard % 2

    def device(dx, dy, dz, dc):
        return ((x + dx) % NX, ((z + dz) % NZ) * 8 + ((y + dy) % NY) * 2 + (c + dc) % 2)

    def first_axis(d):
        return device(d * (1 - c), d * c, 0, 0)

    def last_axis(d):
        return device(d * c, d * (1 - c), 0, 0)

    sibling = device(0, 0, 0, 1)
    quarter = x * (1 - c) + y * c
    other = y * (1 - c) + x * c

    barrier = pltpu.get_barrier_semaphore()
    peers = [device(dx, 0, 0, dc) for dc in range(2) for dx in range(NX) if dx or dc]
    peers += [device(0, d, 0, 0) for d in range(1, NY)]
    peers += [device(0, 0, d, 0) for d in range(1, NZ)]
    for peer in peers:
        pl.semaphore_signal(barrier, inc=1, device_id=peer, device_id_type=MESH)

    columns = [hint(((1 - c) * HALF + k * LOAD) % D, 128) for k in range(D // LOAD)]
    loads = []
    for k, col in enumerate(columns):
        cols = pl.ds(col, LOAD)
        group = []
        for j, (src, dst) in enumerate(((delta, d_buf), (error, e_buf), (basis_t, b_buf))):
            copy = pltpu.make_async_copy(src.at[:, cols], dst.at[:, cols], load_sem.at[k, j])
            copy.start()
            group.append(copy)
        loads.append(group)

    pending = []

    def send(src, dst, sems, index, peer):
        copy = pltpu.make_async_remote_copy(
            src_ref=src, dst_ref=dst, send_sem=sems.at[(0, *index)], recv_sem=sems.at[(1, *index)],
            device_id=peer, device_id_type=MESH,
        )
        copy.start()
        pending.append(copy)
        return copy

    mine = pl.ds(hint(c * ROWS, 8), ROWS)
    part = jnp.zeros((ROWS, RANK), F32)
    moved = None
    for k, col in enumerate(columns):
        for copy in loads[k]:
            copy.wait()
        cols = pl.ds(col, LOAD)
        value = d_buf[:, cols] + e_buf[:, cols]
        merged[:, cols] = value
        if k >= 2:
            mcat[mine, (k - 2) * LOAD : (k - 1) * LOAD] = value
        part = part + dot_nt(value, b_buf[:, cols])
        if k == 1:
            pl.semaphore_wait(barrier, len(peers))
            theirs = pl.ds(hint((1 - c) * HALF, 128), HALF)
            moved = send(merged.at[:, theirs], mcat.at[mine, :], sib_sem, (0,), sibling)

    lbuf[c, x] = jnp.zeros((ROWS, 2 * RANK), F32)
    lbuf[c, x, :, 0:RANK] = part
    lefts = []
    for dx, dc in ((2, 0), (2, 1), (1, 0), (3, 0), (1, 1), (3, 1), (0, 1)):
        lefts.append(send(lbuf.at[c, x], lbuf.at[c, x], left_sem, (dc * 4 + dx,), device(dx, 0, 0, dc)))
    for copy in lefts:
        copy.wait_recv()
    for core in range(2):
        l96[core * ROWS : (core + 1) * ROWS, :] = (
            (lbuf[core, 0] + lbuf[core, 1]) + lbuf[core, 2]
        ) + lbuf[core, 3]
    left = l96[...]
    left_t = jnp.transpose(left)[:RANK, :]
    moved.wait_recv()

    first = []
    for n, (off, width) in enumerate(CHUNKS):
        copies = []
        for d in (2, 1, 3, 0):
            start = hint(((quarter + d) % 4) * QUARTER + off, 128)
            tsend[d, :, off : off + width] = dot(left_t, mcat[:, pl.ds(start, width)])
            if d:
                piece = (d, slice(None), pl.ds(off, width))
                copies.append(send(tsend.at[piece], p1.at[piece], p1_sem, (n, d), first_axis(d)))
        first.append(copies)

    gfull[...] = dot(left_t, left)
    half = pl.ds(hint(c * 32, 32), 32)
    gy[y] = gfull[half, :]
    copies = [send(gy.at[y], gy.at[y], gy_sem, (d,), device(0, d, 0, 0)) for d in (2, 1, 3)]
    for copy in copies:
        copy.wait_recv()
    gz[z] = ((gy[0] + gy[1]) + gy[2]) + gy[3]
    gram_z = [send(gz.at[z], gz.at[z], gz_sem, (d,), device(0, 0, d, 0)) for d in ZORDER]

    second = [None] * len(CHUNKS)
    third = [None] * len(CHUNKS)
    fourth = [None] * len(CHUNKS)
    fifth = [None] * len(CHUNKS)
    base = c * HALF + quarter * QUARTER
    rows = pl.ds(hint(z * 8, 8), 8)

    def stage1(n):
        off, width = CHUNKS[n]
        cols = pl.ds(off, width)
        for copy in first[n]:
            copy.wait_recv()
        s1[:, cols] = ((tsend[0, :, cols] + p1[1, :, cols]) + p1[2, :, cols]) + p1[3, :, cols]
        second[n] = []
        for d in ZORDER:
            out = pl.ds(hint(((z + d) % NZ) * 8, 8), 8)
            second[n].append(send(s1.at[out, cols], p2.at[d, :, cols], p2_sem, (n, d), device(0, 0, d, 0)))

    def stage2(n):
        off, width = CHUNKS[n]
        cols = pl.ds(off, width)
        for copy in second[n]:
            copy.wait_recv()
        value = s1[rows, cols]
        for d in range(1, NZ):
            value = value + p2[d, :, cols]
        p3[other, :, cols] = value
        piece = (other, slice(None), cols)
        third[n] = [send(p3.at[piece], p3.at[piece], p3_sem, (n, d), last_axis(d)) for d in (2, 1, 3)]

    def stage3(n):
        off, width = CHUNKS[n]
        cols = pl.ds(off, width)
        for copy in third[n]:
            copy.wait_recv()
        place = (rows, pl.ds(hint(base + off, 128), width))
        total[place] = ((p3[0, :, cols] + p3[1, :, cols]) + p3[2, :, cols]) + p3[3, :, cols]
        fourth[n] = [send(total.at[place], total.at[place], p4_sem, (n, d), device(0, 0, d, 0)) for d in ZORDER]

    def stage4(n):
        off, width = CHUNKS[n]
        for copy in fourth[n]:
            copy.wait_recv()
        place = (slice(None), pl.ds(hint(base + off, 128), width))
        fifth[n] = [send(total.at[place], total.at[place], p5_sem, (n, d), first_axis(d)) for d in (2, 1, 3)]
        fifth[n].append(send(total.at[place], total.at[place], fwd_sem, (n, 0), sibling))

    def stage5(n):
        off, width = CHUNKS[n]
        for i, d in ((1, 1), (2, 3), (0, 2)):
            fifth[n][i].wait_recv()
            start = hint(c * HALF + ((quarter + 4 - d) % 4) * QUARTER + off, 128)
            place = (slice(None), pl.ds(start, width))
            fifth[n].append(send(total.at[place], total.at[place], fwd_sem, (n, d), sibling))

    def stage6(n):
        for copy in fifth[n][3:]:
            copy.wait_recv()

    def gram_stage():
        for copy in gram_z:
            copy.wait_recv()
        value = gz[0]
        for k in range(1, NZ):
            value = value + gz[k]
        gsum[half, :] = value
        swap = send(gsum.at[half], gsum.at[half], gs_sem, (0,), sibling)
        swap.wait_recv()
        lane = lax.broadcasted_iota(jnp.int32, (RANK, 2 * RANK), 1)
        row = lax.broadcasted_iota(jnp.int32, (RANK, 2 * RANK), 0)
        aug[...] = jnp.where(lane < RANK, gsum[...], jnp.where(lane - RANK == row, 1.0, 0.0))

    def coefficients():
        inverse = pltpu.roll(aug[...], RANK, 1)[:, :RANK]
        own = l96[mine, 0:RANK]
        ortho = dot_nt(own, inverse)
        coef[0:RANK, :] = 0.25 * inverse
        coef[RANK : RANK + ROWS, :] = 0.25 * dot(ortho, inverse)

    count = len(CHUNKS)
    stages = (stage1, stage2, stage3, stage4, stage5, stage6)
    for step in range(len(stages) + count - 1):
        for n in range(count):
            if 0 <= step - n < len(stages):
                stages[step - n](n)
        if step == 0:
            gram_stage()
        elif step == 1:
            eliminate(aug, 0, 32)
        elif step == 2:
            eliminate(aug, 32, RANK)
        elif step == 3:
            coefficients()

    for copy in pending:
        copy.wait_send()


def update_kernel(merged, total, coef, weights, momentum, anchor, new_weights, new_momentum, new_anchor, new_error, new_basis):
    both = dot(coef[...], total[...])
    new_basis[...] = both[:RANK]
    approx = both[RANK:]
    new_error[...] = merged[...] - approx
    moved = nesterov_mu * momentum[...] + approx
    new_momentum[...] = moved
    stepped = weights[...] - outer_rate * (approx + nesterov_mu * moved)
    new_weights[...] = stepped
    new_anchor[...] = anchor_decay * anchor[...] + (1.0 - anchor_decay) * stepped


def per_device(delta, error, weights, momentum, anchor, basis):
    count = len(CHUNKS)
    hbm = pl.BlockSpec(memory_space=pl.ANY)
    vmem = pl.BlockSpec(memory_space=pltpu.VMEM)
    dma = pltpu.SemaphoreType.DMA
    merged, total, coef = pl.pallas_call(
        reduce_kernel,
        out_shape=(
            jax.ShapeDtypeStruct((ROWS, D), F32),
            jax.ShapeDtypeStruct((RANK, D), F32),
            jax.ShapeDtypeStruct((RANK + ROWS, RANK), F32),
        ),
        in_specs=[hbm, hbm, hbm],
        out_specs=(vmem, vmem, vmem),
        scratch_shapes=[
            pltpu.VMEM((ROWS, D), F32),
            pltpu.VMEM((ROWS, D), F32),
            pltpu.VMEM((RANK, D), F32),
            pltpu.VMEM((2 * ROWS, HALF), F32),
            pltpu.VMEM((2, NX, ROWS, 2 * RANK), F32),
            pltpu.VMEM((2 * ROWS, 2 * RANK), F32),
            pltpu.VMEM((4, RANK, QUARTER), F32),
            pltpu.VMEM((4, RANK, QUARTER), F32),
            pltpu.VMEM((RANK, QUARTER), F32),
            pltpu.VMEM((NZ, 8, QUARTER), F32),
            pltpu.VMEM((4, 8, QUARTER), F32),
            pltpu.VMEM((RANK, 2 * RANK), F32),
            pltpu.VMEM((NY, 32, 2 * RANK), F32),
            pltpu.VMEM((NZ, 32, 2 * RANK), F32),
            pltpu.VMEM((RANK, 2 * RANK), F32),
            pltpu.VMEM((RANK, 2 * RANK), F32),
            dma((D // LOAD, 3)),
            dma((2, 1)),
            dma((2, 8)),
            dma((2, count, 4)),
            dma((2, count, 8)),
            dma((2, count, 4)),
            dma((2, count, 8)),
            dma((2, count, 4)),
            dma((2, count, 4)),
            dma((2, 4)),
            dma((2, 8)),
            dma((2, 1)),
        ],
        compiler_params=pltpu.CompilerParams(collective_id=0, has_side_effects=True, vmem_limit_bytes=32 << 20),
    )(delta[0], error[0], basis.T)

    block = 1024

    def cols(height):
        return pl.BlockSpec((height, block), lambda i: (0, i))

    outs = pl.pallas_call(
        update_kernel,
        grid=(D // block,),
        out_shape=[jax.ShapeDtypeStruct((ROWS, D), F32)] * 4 + [jax.ShapeDtypeStruct((RANK, D), F32)],
        in_specs=[cols(ROWS), cols(RANK), pl.BlockSpec((RANK + ROWS, RANK), lambda i: (0, 0)), cols(ROWS), cols(ROWS), cols(ROWS)],
        out_specs=[cols(ROWS)] * 4 + [cols(RANK)],
    )(merged, total, coef, weights, momentum, anchor)
    new_weights, new_momentum, new_anchor, new_error, new_basis = outs
    return (new_weights, new_momentum, new_anchor, new_error[None], new_basis.T)


def solution(mesh):
    in_specs = (
        P("group", "shard", None),
        P("group", "shard", None),
        P("shard", None),
        P("shard", None),
        P("shard", None),
        P(),
    )
    out_specs = (
        P("shard", None),
        P("shard", None),
        P("shard", None),
        P("group", "shard", None),
        P(),
    )
    return jax.shard_map(
        per_device, mesh=mesh, in_specs=in_specs, out_specs=out_specs, check_vma=False
    )
```

```python
import jax
import jax.numpy as jnp
from jax import lax
from jax.experimental import pallas as pl
from jax.experimental.pallas import tpu as pltpu
from jax.sharding import PartitionSpec as P

MESH = pl.DeviceIdType.MESH
HIGHEST = lax.Precision.HIGHEST
F32 = jnp.float32
BF16 = jnp.bfloat16

outer_rate = 0.7
nesterov_mu = 0.9
anchor_decay = 0.9

D = 5120
RANK = 64
ROWS = 48
NX, NY, NZ = 4, 4, 8
HALF = D // 2
QUARTER = HALF // 4
CHUNKS = ((0, 384), (384, 256))
LOAD = 1280
ZORDER = (4, 3, 5, 2, 6, 1, 7)


def hint(value, multiple):
    return pl.multiple_of(value, multiple)


def dot_nt(a, b):
    return lax.dot_general(a, b, (((1,), (1,)), ((), ())), precision=HIGHEST, preferred_element_type=F32)


def dot(a, b):
    return jnp.dot(a, b, precision=HIGHEST, preferred_element_type=F32)


def split(value):
    high = value.astype(BF16)
    return high, (value - high.astype(F32)).astype(BF16)


def bdot(a, b):
    return jnp.dot(a, b, preferred_element_type=F32)


def eliminate(aug, first, last):
    for j in range(first, last):
        block = j // 8 * 8
        pivot = aug[j : j + 1, j : j + 1]
        scale = lax.rsqrt(pivot)
        scale = scale * (1.5 - 0.5 * pivot * scale * scale)
        row = aug[j : j + 1, :] * scale
        tail = aug[block:, :]
        index = lax.broadcasted_iota(jnp.int32, tail.shape, 0) + block
        moved = tail - (tail[:, j : j + 1] * scale) * row
        tail = jnp.where(index > j, moved, jnp.where(index == j, row, tail))
        aug[block:, :] = tail


def step_kernel(
    delta, error, basis_t, weights, momentum, anchor,
    new_weights, new_momentum, new_anchor, new_error, new_basis,
    d_buf, e_buf, b_buf, w_buf, m_buf, a_buf, merged, total, coef, msib, mst, lbuf, l96, tsend, p1, s1, p2, p3, gfull, gy, gz, gsum, aug,
    load_sem, late_sem, sib_sem, left_sem, p1_sem, p2_sem, p3_sem, p4_sem, p5_sem, fwd_sem, gy_sem, gz_sem, gs_sem,
):
    x = lax.axis_index("group")
    shard = lax.axis_index("shard")
    z = shard // 8
    y = (shard // 2) % 4
    c = shard % 2

    def device(dx, dy, dz, dc):
        return ((x + dx) % NX, ((z + dz) % NZ) * 8 + ((y + dy) % NY) * 2 + (c + dc) % 2)

    def first_axis(d):
        return device(d * (1 - c), d * c, 0, 0)

    def last_axis(d):
        return device(d * c, d * (1 - c), 0, 0)

    sibling = device(0, 0, 0, 1)
    quarter = x * (1 - c) + y * c
    other = y * (1 - c) + x * c

    columns = [hint(((1 - c) * HALF + k * LOAD) % D, 128) for k in range(D // LOAD)]
    loads = []
    for k, col in enumerate(columns):
        cols = pl.ds(col, LOAD)
        group = []
        for j, (src, dst) in enumerate(((delta, d_buf), (error, e_buf), (basis_t, b_buf))):
            copy = pltpu.make_async_copy(src.at[:, cols], dst.at[:, cols], load_sem.at[k, j])
            copy.start()
            group.append(copy)
        loads.append(group)

    barrier = pltpu.get_barrier_semaphore()
    peers = [device(0, 0, d, 0) for d in ZORDER]
    peers += [device(dx, 0, 0, dc) for dc in range(2) for dx in range(NX) if dx or dc]
    peers += [device(0, d, 0, 0) for d in range(1, NY)]
    for peer in peers:
        pl.semaphore_signal(barrier, inc=1, device_id=peer, device_id_type=MESH)

    late = []
    for j, (src, dst) in enumerate(((weights, w_buf), (momentum, m_buf), (anchor, a_buf))):
        copy = pltpu.make_async_copy(src, dst, late_sem.at[j])
        copy.start()
        late.append(copy)

    pending = []

    def send(src, dst, sems, index, peer):
        copy = pltpu.make_async_remote_copy(
            src_ref=src, dst_ref=dst, send_sem=sems.at[(0, *index)], recv_sem=sems.at[(1, *index)],
            device_id=peer, device_id_type=MESH,
        )
        copy.start()
        pending.append(copy)
        return copy

    mine = pl.ds(hint(c * ROWS, 16), ROWS)
    mine_low = pl.ds(hint((2 + c) * ROWS, 16), ROWS)
    theirs = pl.ds(hint((1 - c) * ROWS, 16), ROWS)
    theirs_low = pl.ds(hint((3 - c) * ROWS, 16), ROWS)
    part = jnp.zeros((2 * ROWS, 2 * RANK), F32)
    for k, col in enumerate(columns):
        for copy in loads[k]:
            copy.wait()
        cols = pl.ds(col, LOAD)
        value = d_buf[:, cols] + e_buf[:, cols]
        merged[:, cols] = value
        high, low = split(value)
        if k >= 2:
            mst[mine, (k - 2) * LOAD : (k - 1) * LOAD] = high
            mst[mine_low, (k - 2) * LOAD : (k - 1) * LOAD] = low
        part = part + lax.dot_general(
            jnp.concatenate([high, low], axis=0), jnp.concatenate(split(b_buf[:, cols]), axis=0),
            (((1,), (1,)), ((), ())), preferred_element_type=F32,
        )
    pl.semaphore_wait(barrier, len(peers))
    lane = lax.broadcasted_iota(jnp.int32, (ROWS, 2 * RANK), 1)
    rows_sum = part[:ROWS] + part[ROWS:]
    lbuf[c, x] = jnp.where(lane < RANK, rows_sum + pltpu.roll(rows_sum, RANK, 1), 0.0)

    lefts = []
    for dx, dc in ((2, 0), (2, 1), (1, 0), (3, 0), (1, 1), (3, 1), (0, 1)):
        lefts.append(send(lbuf.at[c, x], lbuf.at[c, x], left_sem, (dc * 4 + dx,), device(dx, 0, 0, dc)))
    away = pl.ds(hint((1 - c) * HALF, 128), HALF)
    moved = send(merged.at[:, away], msib, sib_sem, (0,), sibling)
    moved.wait_recv()
    mst[theirs, :], mst[theirs_low, :] = split(msib[...])
    for copy in lefts:
        copy.wait_recv()
    for core in range(2):
        l96[core * ROWS : (core + 1) * ROWS, :] = (
            (lbuf[core, 0] + lbuf[core, 1]) + lbuf[core, 2]
        ) + lbuf[core, 3]
    left = l96[...]
    left_high = left.astype(BF16).astype(F32)
    pair = left_high + pltpu.roll(left - left_high, RANK, 1)
    left_t = jnp.transpose(jnp.concatenate([pair, pair], axis=0)).astype(BF16)

    first = []
    for n, (off, width) in enumerate(CHUNKS):
        copies = []
        for d in (2, 1, 3, 0):
            start = hint(((quarter + d) % 4) * QUARTER + off, 128)
            term = bdot(left_t, mst[:, pl.ds(start, width)])
            tsend[d, :, off : off + width] = term[:RANK] + term[RANK:]
            if d:
                piece = (d, slice(None), pl.ds(off, width))
                copies.append(send(tsend.at[piece], p1.at[piece], p1_sem, (n, d), first_axis(d)))
        first.append(copies)

    gfull[...] = dot(jnp.transpose(left)[:RANK], left)
    half = pl.ds(hint(c * 32, 32), 32)
    gy[y] = gfull[half, :]
    gram_y = [send(gy.at[y], gy.at[y], gy_sem, (d,), device(0, d, 0, 0)) for d in (2, 1, 3)]

    second = [None] * len(CHUNKS)
    third = [None] * len(CHUNKS)
    fourth = [None] * len(CHUNKS)
    fifth = [None] * len(CHUNKS)
    sixth = [None] * len(CHUNKS)
    base = c * HALF + quarter * QUARTER
    rows = pl.ds(hint(z * 8, 8), 8)

    def scatter_z(n):
        off, width = CHUNKS[n]
        cols = pl.ds(off, width)
        for copy in first[n]:
            copy.wait_recv()
        s1[:, cols] = ((tsend[0, :, cols] + p1[1, :, cols]) + p1[2, :, cols]) + p1[3, :, cols]
        second[n] = []
        for d in ZORDER:
            out = pl.ds(hint(((z + d) % NZ) * 8, 8), 8)
            second[n].append(send(s1.at[out, cols], p2.at[d, :, cols], p2_sem, (n, d), device(0, 0, d, 0)))

    def sum_last(n):
        off, width = CHUNKS[n]
        cols = pl.ds(off, width)
        for copy in second[n]:
            copy.wait_recv()
        value = s1[rows, cols]
        for d in range(1, NZ):
            value = value + p2[d, :, cols]
        p3[other, :, cols] = value
        piece = (other, slice(None), cols)
        third[n] = [send(p3.at[piece], p3.at[piece], p3_sem, (n, d), last_axis(d)) for d in (2, 1, 3)]

    def gather_z(n):
        off, width = CHUNKS[n]
        cols = pl.ds(off, width)
        for copy in third[n]:
            copy.wait_recv()
        place = (rows, pl.ds(hint(base + off, 128), width))
        total[place] = ((p3[0, :, cols] + p3[1, :, cols]) + p3[2, :, cols]) + p3[3, :, cols]
        fourth[n] = [send(total.at[place], total.at[place], p4_sem, (n, d), device(0, 0, d, 0)) for d in ZORDER]

    def gather_first(n):
        off, width = CHUNKS[n]
        for copy in fourth[n]:
            copy.wait_recv()
        place = (slice(None), pl.ds(hint(base + off, 128), width))
        fifth[n] = [(d, send(total.at[place], total.at[place], p5_sem, (n, d), first_axis(d))) for d in (2, 1, 3)]
        sixth[n] = [(0, send(total.at[place], total.at[place], fwd_sem, (n, 0), sibling))]

    def gather_core(n):
        off, width = CHUNKS[n]
        for i in (1, 2, 0):
            d, copy = fifth[n][i]
            copy.wait_recv()
            start = hint(c * HALF + ((quarter + 4 - d) % 4) * QUARTER + off, 128)
            place = (slice(None), pl.ds(start, width))
            sixth[n].append((d, send(total.at[place], total.at[place], fwd_sem, (n, d), sibling)))

    def gram_rest():
        for copy in gram_y:
            copy.wait_recv()
        gz[z] = ((gy[0] + gy[1]) + gy[2]) + gy[3]
        return [send(gz.at[z], gz.at[z], gz_sem, (d,), device(0, 0, d, 0)) for d in ZORDER]

    def gram_swap(copies):
        for copy in copies:
            copy.wait_recv()
        value = gz[0]
        for k in range(1, NZ):
            value = value + gz[k]
        gsum[half, :] = value
        return send(gsum.at[half], gsum.at[half], gs_sem, (0,), sibling)

    def factor():
        lane = lax.broadcasted_iota(jnp.int32, (RANK, 2 * RANK), 1)
        row = lax.broadcasted_iota(jnp.int32, (RANK, 2 * RANK), 0)
        aug[...] = jnp.where(lane < RANK, gsum[...], jnp.where(lane - RANK == row, 1.0, 0.0))
        eliminate(aug, 0, RANK)
        inverse = pltpu.roll(aug[...], RANK, 1)[:, :RANK]
        own = l96[pl.ds(hint(c * ROWS, 8), ROWS), 0:RANK]
        ortho = dot_nt(own, inverse)
        both = 0.25 * jnp.concatenate([inverse, dot(ortho, inverse)], axis=0)
        high, low = split(both)
        coef[...] = jnp.concatenate([high, high, low, low], axis=1)

    def update(start, width):
        cols = pl.ds(start, width)
        high, low = split(total[:, cols])
        both = bdot(coef[...], jnp.concatenate([high, low, high, low], axis=0))
        new_basis[:, cols] = both[:RANK]
        approx = both[RANK:]
        new_error[:, cols] = merged[:, cols] - approx
        speed = nesterov_mu * m_buf[:, cols] + approx
        new_momentum[:, cols] = speed
        stepped = w_buf[:, cols] - outer_rate * (approx + nesterov_mu * speed)
        new_weights[:, cols] = stepped
        new_anchor[:, cols] = anchor_decay * a_buf[:, cols] + (1.0 - anchor_decay) * stepped

    everything = range(len(CHUNKS))
    scatter_z(0)
    gram_z = gram_rest()
    for n in everything[1:]:
        scatter_z(n)
    for n in everything:
        sum_last(n)
    swap = gram_swap(gram_z)
    for n in everything:
        gather_z(n)
    swap.wait_recv()
    factor()
    for copy in late:
        copy.wait()
    for n in everything:
        gather_first(n)
    update(hint(base, 128), QUARTER)
    for n in everything:
        gather_core(n)
    for d in (1, 3, 2):
        update(hint(c * HALF + ((quarter + 4 - d) % 4) * QUARTER, 128), QUARTER)
    there = y * (1 - c) + x * c
    for d in (0, 1, 3, 2):
        for n in everything:
            for key, copy in sixth[n]:
                if key == d:
                    copy.wait_recv()
        update(hint((1 - c) * HALF + ((there + 4 - d) % 4) * QUARTER, 128), QUARTER)

    for copy in pending:
        copy.wait_send()


def store_kernel(*refs):
    sems = refs[-1]
    count = len(refs) // 2
    copies = [pltpu.make_async_copy(refs[k], refs[count + k], sems.at[k]) for k in range(count)]
    for copy in copies:
        copy.start()
    for copy in copies:
        copy.wait()


def per_device(delta, error, weights, momentum, anchor, basis):
    count = len(CHUNKS)
    hbm = pl.BlockSpec(memory_space=pltpu.HBM)
    vmem = pl.BlockSpec(memory_space=pltpu.VMEM)
    dma = pltpu.SemaphoreType.DMA
    shapes = [jax.ShapeDtypeStruct((ROWS, D), F32)] * 4 + [jax.ShapeDtypeStruct((RANK, D), F32)]
    outs = pl.pallas_call(
        step_kernel,
        out_shape=shapes,
        in_specs=[hbm] * 6,
        out_specs=[vmem] * 5,
        scratch_shapes=[
            pltpu.VMEM((ROWS, D), F32),
            pltpu.VMEM((ROWS, D), F32),
            pltpu.VMEM((RANK, D), F32),
            pltpu.VMEM((ROWS, D), F32),
            pltpu.VMEM((ROWS, D), F32),
            pltpu.VMEM((ROWS, D), F32),
            pltpu.VMEM((ROWS, D), F32),
            pltpu.VMEM((RANK, D), F32),
            pltpu.VMEM((RANK + ROWS, 4 * RANK), BF16),
            pltpu.VMEM((ROWS, HALF), F32),
            pltpu.VMEM((4 * ROWS, HALF), BF16),
            pltpu.VMEM((2, NX, ROWS, 2 * RANK), F32),
            pltpu.VMEM((2 * ROWS, 2 * RANK), F32),
            pltpu.VMEM((4, RANK, QUARTER), F32),
            pltpu.VMEM((4, RANK, QUARTER), F32),
            pltpu.VMEM((RANK, QUARTER), F32),
            pltpu.VMEM((NZ, 8, QUARTER), F32),
            pltpu.VMEM((4, 8, QUARTER), F32),
            pltpu.VMEM((RANK, 2 * RANK), F32),
            pltpu.VMEM((NY, 32, 2 * RANK), F32),
            pltpu.VMEM((NZ, 32, 2 * RANK), F32),
            pltpu.VMEM((RANK, 2 * RANK), F32),
            pltpu.VMEM((RANK, 2 * RANK), F32),
            dma((D // LOAD, 3)),
            dma((3,)),
            dma((2, 1)),
            dma((2, 8)),
            dma((2, count, 4)),
            dma((2, count, 8)),
            dma((2, count, 4)),
            dma((2, count, 8)),
            dma((2, count, 4)),
            dma((2, count, 4)),
            dma((2, 4)),
            dma((2, 8)),
            dma((2, 1)),
        ],
        compiler_params=pltpu.CompilerParams(collective_id=0, has_side_effects=True, vmem_limit_bytes=32 << 20),
    )(*(pltpu.with_memory_space_constraint(a, pltpu.HBM) for a in (delta[0], error[0], basis.T, weights, momentum, anchor)))
    outs = pl.pallas_call(
        store_kernel,
        out_shape=shapes,
        in_specs=[vmem] * 5,
        out_specs=[hbm] * 5,
        scratch_shapes=[dma((5,))],
        compiler_params=pltpu.CompilerParams(vmem_limit_bytes=1 << 20),
    )(*(pltpu.with_memory_space_constraint(a, pltpu.VMEM) for a in outs))
    new_weights, new_momentum, new_anchor, new_error, new_basis = outs
    return (new_weights, new_momentum, new_anchor, new_error[None], new_basis.T)


def solution(mesh):
    in_specs = (
        P("group", "shard", None),
        P("group", "shard", None),
        P("shard", None),
        P("shard", None),
        P("shard", None),
        P(),
    )
    out_specs = (
        P("shard", None),
        P("shard", None),
        P("shard", None),
        P("group", "shard", None),
        P(),
    )
    return jax.shard_map(
        per_device, mesh=mesh, in_specs=in_specs, out_specs=out_specs, check_vma=False
    )
```

```python
import jax
import jax.numpy as jnp
from jax import lax
from jax.experimental import pallas as pl
from jax.experimental.pallas import tpu as pltpu
from jax.sharding import PartitionSpec as P

MESH = pl.DeviceIdType.MESH
HIGHEST = lax.Precision.HIGHEST
F32 = jnp.float32
BF16 = jnp.bfloat16

outer_rate = 0.7
nesterov_mu = 0.9
anchor_decay = 0.9

D = 5120
RANK = 64
ROWS = 48
NX, NY, NZ = 4, 4, 8
HALF = D // 2
PLANE = 896
ZFIRST = HALF - 2 * PLANE
CHUNKS = ((True, 0, 384), (False, 0, 512), (True, 384, 384), (False, 512, 384))
LOAD = 1280
ZORDER = (4, 3, 5, 2, 6, 1, 7)
PLANEORDER = ((2, 0), (2, 1), (1, 0), (3, 0), (1, 1), (3, 1), (0, 1))
XYORDER = ((2, 2), (2, 1), (2, 3), (1, 2), (3, 2), (2, 0), (0, 2), (1, 1), (1, 3), (3, 1), (3, 3), (1, 0), (3, 0), (0, 1), (0, 3))


def hint(value, multiple):
    return pl.multiple_of(value, multiple)


def dot_nt(a, b):
    return lax.dot_general(a, b, (((1,), (1,)), ((), ())), precision=HIGHEST, preferred_element_type=F32)


def dot(a, b):
    return jnp.dot(a, b, precision=HIGHEST, preferred_element_type=F32)


def split(value):
    high = value.astype(BF16)
    return high, (value - high.astype(F32)).astype(BF16)


def bdot(a, b):
    return jnp.dot(a, b, preferred_element_type=F32)


def eliminate(blocks, first, last):
    index = lax.broadcasted_iota(jnp.int32, (8, 1), 0)
    for j in range(first, last):
        own = j // 8
        row = blocks[own][j % 8 : j % 8 + 1, :]
        row = row * (1.0 / row[:, j : j + 1])
        for k in range(own, RANK // 8):
            column = blocks[k][:, j : j + 1]
            if k == own:
                column = jnp.where(index > j % 8, column, 0.0)
            blocks[k] = blocks[k] - column * row
    return blocks


def step_kernel(
    delta, error, basis_t, weights, momentum, anchor,
    new_weights, new_momentum, new_anchor, new_error, new_basis,
    d_buf, e_buf, b_buf, w_buf, m_buf, a_buf, merged, total, coef, msib, mst, lbuf, l96, term, ra1, rc1, ra2, rc2, gfull, gy, gz, gx,
    load_sem, late_sem, sib_sem, left_sem, sem1, sem2, sem3, fwd_sem, gram_sem,
):
    x = lax.axis_index("group")
    shard = lax.axis_index("shard")
    z = lax.div(shard, 8)
    y = lax.rem(lax.div(shard, 2), 4)
    c = lax.rem(shard, 2)
    plane = x * NY + y

    xs = [lax.rem(x + d, NX) for d in range(NX)]
    ys = [lax.rem(y + d, NY) for d in range(NY)]
    zs = [lax.rem(z + d, NZ) for d in range(NZ)]
    cs = [c, 1 - c]
    known = {}

    def device(dx, dy, dz, dc):
        key = (dx, dy, dz, dc)
        if key not in known:
            known[key] = (xs[dx], zs[dz] * 8 + ys[dy] * 2 + cs[dc])
        return known[key]

    sibling = device(0, 0, 0, 1)

    barrier = pltpu.get_barrier_semaphore()
    peers = [device(0, 0, d, 0) for d in ZORDER]
    peers += [device(dx, dy, 0, 0) for dx, dy in XYORDER]
    peers += [device(dx, 0, 0, 1) for dx in (2, 1, 3, 0)]
    for peer in peers:
        pl.semaphore_signal(barrier, inc=1, device_id=peer, device_id_type=MESH)

    columns = [hint(((1 - c) * HALF + k * LOAD) % D, 128) for k in range(D // LOAD)]
    loads = []
    for k, col in enumerate(columns):
        cols = pl.ds(col, LOAD)
        group = []
        for j, (src, dst) in enumerate(((delta, d_buf), (error, e_buf), (basis_t, b_buf))):
            copy = pltpu.make_async_copy(src.at[:, cols], dst.at[:, cols], load_sem.at[k, j])
            copy.start()
            group.append(copy)
        loads.append(group)

    late = []
    for j, (src, dst) in enumerate(((weights, w_buf), (momentum, m_buf), (anchor, a_buf))):
        copy = pltpu.make_async_copy(src, dst, late_sem.at[j])
        copy.start()
        late.append(copy)

    pending = []

    def link(src, dst, sems, n, peer):
        return pltpu.make_async_remote_copy(
            src_ref=src, dst_ref=dst, send_sem=sems.at[0, n], recv_sem=sems.at[1, n],
            device_id=peer, device_id_type=MESH,
        )

    def send_all(pieces, sems, n, like):
        for src, dst, peer in pieces:
            link(src, dst, sems, n, peer).start()
        copy = link(like, like, sems, n, sibling)
        pending.append(copy)
        return copy

    mine = pl.ds(hint(c * ROWS, 16), ROWS)
    mine_low = pl.ds(hint((2 + c) * ROWS, 16), ROWS)
    theirs = pl.ds(hint((1 - c) * ROWS, 16), ROWS)
    theirs_low = pl.ds(hint((3 - c) * ROWS, 16), ROWS)
    part = jnp.zeros((2 * ROWS, 2 * RANK), F32)
    for k, col in enumerate(columns):
        for copy in loads[k]:
            copy.wait()
        cols = pl.ds(col, LOAD)
        value = d_buf[:, cols] + e_buf[:, cols]
        merged[:, cols] = value
        high, low = split(value)
        if k >= 2:
            mst[mine, (k - 2) * LOAD : (k - 1) * LOAD] = high
            mst[mine_low, (k - 2) * LOAD : (k - 1) * LOAD] = low
        part = part + lax.dot_general(
            jnp.concatenate([high, low], axis=0), jnp.concatenate(split(b_buf[:, cols]), axis=0),
            (((1,), (1,)), ((), ())), preferred_element_type=F32,
        )
    pl.semaphore_wait(barrier, len(peers))
    part = part[:ROWS] + part[ROWS:]
    part = part + pltpu.roll(part, RANK, 1)
    low_lanes = lax.broadcasted_iota(jnp.int32, (ROWS // 2, 2 * RANK), 1) < RANK
    lbuf[c * NX + x] = jnp.where(low_lanes, part[: ROWS // 2], part[ROWS // 2 :])

    slot = lbuf.at[c * NX + x]
    lefts = send_all([(slot, slot, device(dx, 0, 0, dc)) for dx, dc in PLANEORDER], left_sem, 0, lbuf.at[0:7])
    away = merged.at[:, pl.ds(hint((1 - c) * HALF, 128), HALF)]
    moved = send_all([(away, msib, sibling)], sib_sem, 0, msib)
    moved.wait_recv()
    mst[theirs, :], mst[theirs_low, :] = split(msib[...])
    lefts.wait_recv()
    for core in range(2):
        packed = ((lbuf[core * NX] + lbuf[core * NX + 1]) + lbuf[core * NX + 2]) + lbuf[core * NX + 3]
        l96[core * ROWS : core * ROWS + ROWS // 2, :] = jnp.where(low_lanes, packed, 0.0)
        l96[core * ROWS + ROWS // 2 : (core + 1) * ROWS, :] = jnp.where(low_lanes, pltpu.roll(packed, RANK, 1), 0.0)
    left = l96[...]
    left_high = left.astype(BF16).astype(F32)
    pair = left_high + pltpu.roll(left - left_high, RANK, 1)
    left_t = jnp.transpose(jnp.concatenate([pair, pair], axis=0)).astype(BF16)

    def terms(start, width):
        value = bdot(left_t, mst[:, start : start + width])
        term[:, start : start + width] = value[:RANK] + value[RANK:]

    count = len(CHUNKS)
    z_rows = pl.ds(hint(z * 8, 8), 8)
    plane_rows = pl.ds(hint(lax.div(plane, 2) * 8, 8), 8)
    plane_col = lax.rem(plane, 2) * PLANE
    out_rows = [pl.ds(hint(zs[d] * 8, 8), 8) for d in range(NZ)]
    out_plane = {}
    for dx, dy in XYORDER:
        piece = xs[dx] * NY + ys[dy]
        out_plane[dx, dy] = (pl.ds(hint(lax.div(piece, 2) * 8, 8), 8), lax.rem(piece, 2) * PLANE)

    def over_z(src, dst, sems, n, like):
        return send_all([(src, dst, device(0, 0, d, 0)) for d in ZORDER], sems, n, like)

    def over_xy(src, dst, sems, n, like):
        return send_all([(src, dst, device(dx, dy, 0, 0)) for dx, dy in XYORDER], sems, n, like)

    def stage0(n):
        zfirst, off, width = CHUNKS[n]
        cols = pl.ds(off, width)
        if zfirst:
            start = 2 * PLANE + off
            terms(start, width)
            pieces = [(term.at[out_rows[d], pl.ds(start, width)], rc1.at[d, :, cols], device(0, 0, d, 0)) for d in ZORDER]
            return send_all(pieces, sem1, n, rc1.at[1:NZ, :, cols])
        for side in range(2):
            terms(side * PLANE + off, width)
        pieces = []
        for dx, dy in XYORDER:
            rows, col = out_plane[dx, dy]
            src = term.at[rows, pl.ds(hint(col + off, 128), width)]
            pieces.append((src, ra1.at[dx * NY + dy, :, cols], device(dx, dy, 0, 0)))
        return send_all(pieces, sem1, n, ra1.at[1 : NX * NY, :, cols])

    def stage1(n):
        zfirst, off, width = CHUNKS[n]
        cols = pl.ds(off, width)
        first[n].wait_recv()
        if zfirst:
            value = term[z_rows, pl.ds(2 * PLANE + off, width)]
            for d in range(1, NZ):
                value = value + rc1[d, :, cols]
            rc2[plane, :, cols] = value
            piece = rc2.at[plane, :, cols]
            return over_xy(piece, piece, sem2, n, rc2.at[1 : NX * NY, :, cols])
        value = term[plane_rows, pl.ds(hint(plane_col + off, 128), width)]
        for d in range(1, NX * NY):
            value = value + ra1[d, :, cols]
        ra2[z, :, cols] = value
        piece = ra2.at[z, :, cols]
        return over_z(piece, piece, sem2, n, ra2.at[1:NZ, :, cols])

    def stage2(n):
        zfirst, off, width = CHUNKS[n]
        cols = pl.ds(off, width)
        second[n].wait_recv()
        if zfirst:
            value = rc2[0, :, cols]
            for k in range(1, NX * NY):
                value = value + rc2[k, :, cols]
            place = (z_rows, pl.ds(hint(c * HALF + 2 * PLANE + off, 128), width))
            total[place] = value
            return over_z(total.at[place], total.at[place], sem3, n, rc1.at[1:NZ, :, cols])
        value = ra2[0, :, cols]
        for k in range(1, NZ):
            value = value + ra2[k, :, cols]
        place = (plane_rows, pl.ds(hint(c * HALF + plane_col + off, 128), width))
        total[place] = value
        return over_xy(total.at[place], total.at[place], sem3, n, ra1.at[1 : NX * NY, :, cols])

    def ranges(n, core):
        zfirst, off, width = CHUNKS[n]
        starts = (2 * PLANE + off,) if zfirst else (off, PLANE + off)
        return [pl.ds(hint(core * HALF + start, 128), width) for start in starts]

    def stage3(n):
        third[n].wait_recv()
        places = [total.at[:, cols] for cols in ranges(n, c)]
        return send_all([(p, p, sibling) for p in places], fwd_sem, n, term.at[:, 0 : len(places) * CHUNKS[n][2]])

    share = x * 2 + c

    def gram_start():
        gfull[...] = dot(jnp.transpose(left)[:RANK], left)
        gy[y] = gfull[pl.ds(hint(share * 8, 8), 8), :]
        pieces = [(gy.at[y], gy.at[y], device(0, d, 0, 0)) for d in (2, 1, 3)]
        return send_all(pieces, gram_sem, 0, gy.at[1:NY])

    def gram_middle(copies):
        copies.wait_recv()
        gz[z] = ((gy[0] + gy[1]) + gy[2]) + gy[3]
        return over_z(gz.at[z], gz.at[z], gram_sem, 1, gz.at[1:NZ])

    def gram_end(copies):
        copies.wait_recv()
        value = gz[0]
        for k in range(1, NZ):
            value = value + gz[k]
        gx[share] = value
        pieces = [(gx.at[share], gx.at[share], device(dx, 0, 0, dc)) for dx, dc in PLANEORDER]
        return send_all(pieces, gram_sem, 2, gx.at[1:8])

    def gram_blocks():
        lane = lax.broadcasted_iota(jnp.int32, (8, 2 * RANK), 1)
        row = lax.broadcasted_iota(jnp.int32, (8, 2 * RANK), 0)
        return [
            jnp.where(lane < RANK, gx[k], jnp.where(lane == row + (RANK + 8 * k), 1.0, 0.0)) for k in range(RANK // 8)
        ]

    def coefficients(blocks):
        whole = jnp.concatenate(blocks, axis=0)
        lane = lax.broadcasted_iota(jnp.int32, (RANK, 2 * RANK), 1)
        row = lax.broadcasted_iota(jnp.int32, (RANK, 2 * RANK), 0)
        pivot = jnp.sum(jnp.where(lane == row, whole, 0.0), axis=1, keepdims=True)
        scale = lax.rsqrt(pivot)
        scale = scale * (1.5 - 0.5 * pivot * scale * scale)
        inverse = (pltpu.roll(whole, RANK, 1) * scale)[:, :RANK]
        own = l96[pl.ds(hint(c * ROWS, 8), ROWS), 0:RANK]
        ortho = dot_nt(own, inverse)
        both = 0.25 * jnp.concatenate([inverse, dot(ortho, inverse)], axis=0)
        high, low = split(both)
        coef[...] = jnp.concatenate([high, high, low, low], axis=1)

    def update(cols):
        high, low = split(total[:, cols])
        both = bdot(coef[...], jnp.concatenate([high, low, high, low], axis=0))
        new_basis[:, cols] = both[:RANK]
        approx = both[RANK:]
        new_error[:, cols] = merged[:, cols] - approx
        speed = nesterov_mu * m_buf[:, cols] + approx
        new_momentum[:, cols] = speed
        stepped = w_buf[:, cols] - outer_rate * (approx + nesterov_mu * speed)
        new_weights[:, cols] = stepped
        new_anchor[:, cols] = anchor_decay * a_buf[:, cols] + (1.0 - anchor_decay) * stepped

    def update_own(n):
        for cols in ranges(n, c):
            update(cols)

    def update_sibling(n):
        fourth[n].wait_recv()
        for cols in ranges(n, 1 - c):
            update(cols)

    early = count // 2
    first = [stage0(n) for n in range(early)]
    gram = gram_start()
    first += [stage0(n) for n in range(early, count)]
    gram = gram_middle(gram)
    second = [stage1(n) for n in range(early)]
    gram = gram_end(gram)
    second += [stage1(n) for n in range(early, count)]
    gram.wait_recv()
    blocks = eliminate(gram_blocks(), 0, 32)
    third = [stage2(n) for n in range(count)]
    coefficients(eliminate(blocks, 32, RANK))
    for copy in late:
        copy.wait()
    fourth = []
    for n in range(count):
        fourth.append(stage3(n))
        if n:
            update_own(n - 1)
    for n in range(count - 1):
        update_sibling(n)
    update_own(count - 1)
    update_sibling(count - 1)
    for copy in pending:
        copy.wait_send()


def store_kernel(*refs):
    sems = refs[-1]
    count = len(refs) // 2
    copies = [pltpu.make_async_copy(refs[k], refs[count + k], sems.at[k]) for k in range(count)]
    for copy in copies:
        copy.start()
    for copy in copies:
        copy.wait()


def per_device(delta, error, weights, momentum, anchor, basis):
    count = len(CHUNKS)
    hbm = pl.BlockSpec(memory_space=pltpu.HBM)
    vmem = pl.BlockSpec(memory_space=pltpu.VMEM)
    dma = pltpu.SemaphoreType.DMA
    shapes = [jax.ShapeDtypeStruct((ROWS, D), F32)] * 4 + [jax.ShapeDtypeStruct((RANK, D), F32)]
    outs = pl.pallas_call(
        step_kernel,
        out_shape=shapes,
        in_specs=[hbm] * 6,
        out_specs=[vmem] * 5,
        scratch_shapes=[
            pltpu.VMEM((ROWS, D), F32),
            pltpu.VMEM((ROWS, D), F32),
            pltpu.VMEM((RANK, D), F32),
            pltpu.VMEM((ROWS, D), F32),
            pltpu.VMEM((ROWS, D), F32),
            pltpu.VMEM((ROWS, D), F32),
            pltpu.VMEM((ROWS, D), F32),
            pltpu.VMEM((RANK, D), F32),
            pltpu.VMEM((RANK + ROWS, 4 * RANK), BF16),
            pltpu.VMEM((ROWS, HALF), F32),
            pltpu.VMEM((4 * ROWS, HALF), BF16),
            pltpu.VMEM((2 * NX, ROWS // 2, 2 * RANK), F32),
            pltpu.VMEM((2 * ROWS, 2 * RANK), F32),
            pltpu.VMEM((RANK, HALF), F32),
            pltpu.VMEM((NX * NY, 8, PLANE), F32),
            pltpu.VMEM((NZ, 8, ZFIRST), F32),
            pltpu.VMEM((NZ, 8, PLANE), F32),
            pltpu.VMEM((NX * NY, 8, ZFIRST), F32),
            pltpu.VMEM((RANK, 2 * RANK), F32),
            pltpu.VMEM((NY, 8, 2 * RANK), F32),
            pltpu.VMEM((NZ, 8, 2 * RANK), F32),
            pltpu.VMEM((8, 8, 2 * RANK), F32),
            dma((D // LOAD, 3)),
            dma((3,)),
            dma((2, 1)),
            dma((2, 1)),
            dma((2, count)),
            dma((2, count)),
            dma((2, count)),
            dma((2, count)),
            dma((2, 3)),
        ],
        compiler_params=pltpu.CompilerParams(collective_id=0, has_side_effects=True, vmem_limit_bytes=32 << 20),
    )(*(pltpu.with_memory_space_constraint(a, pltpu.HBM) for a in (delta[0], error[0], basis.T, weights, momentum, anchor)))
    outs = pl.pallas_call(
        store_kernel,
        out_shape=shapes,
        in_specs=[vmem] * 5,
        out_specs=[hbm] * 5,
        scratch_shapes=[dma((5,))],
        compiler_params=pltpu.CompilerParams(vmem_limit_bytes=1 << 20),
    )(*(pltpu.with_memory_space_constraint(a, pltpu.VMEM) for a in outs))
    new_weights, new_momentum, new_anchor, new_error, new_basis = outs
    return (new_weights, new_momentum, new_anchor, new_error[None], new_basis.T)


def solution(mesh):
    in_specs = (
        P("group", "shard", None),
        P("group", "shard", None),
        P("shard", None),
        P("shard", None),
        P("shard", None),
        P(),
    )
    out_specs = (
        P("shard", None),
        P("shard", None),
        P("shard", None),
        P("group", "shard", None),
        P(),
    )
    return jax.shard_map(
        per_device, mesh=mesh, in_specs=in_specs, out_specs=out_specs, check_vma=False
    )
```

```python
import jax
import jax.numpy as jnp
from jax import lax
from jax.experimental import pallas as pl
from jax.experimental.pallas import tpu as pltpu
from jax.sharding import PartitionSpec as P

MESH = pl.DeviceIdType.MESH
HIGHEST = lax.Precision.HIGHEST
F32 = jnp.float32
BF16 = jnp.bfloat16

outer_rate = 0.7
nesterov_mu = 0.9
anchor_decay = 0.9

D = 5120
RANK = 64
ROWS = 48
NX, NY, NZ = 4, 4, 8
HALF = D // 2
PLANE = 896
ZFIRST = HALF - 2 * PLANE
CHUNKS = ((True, 0, 384), (False, 0, 512), (True, 384, 384), (False, 512, 384))
LOAD = 1280
GROUP = 4
ZORDER = (4, 3, 5, 2, 6, 1, 7)
PLANEORDER = ((2, 0), (2, 1), (1, 0), (3, 0), (1, 1), (3, 1), (0, 1))
XYORDER = ((2, 2), (2, 1), (2, 3), (1, 2), (3, 2), (2, 0), (0, 2), (1, 1), (1, 3), (3, 1), (3, 3), (1, 0), (3, 0), (0, 1), (0, 3))


def hint(value, multiple):
    return pl.multiple_of(value, multiple)


def dot_nt(a, b):
    return lax.dot_general(a, b, (((1,), (1,)), ((), ())), precision=HIGHEST, preferred_element_type=F32)


def dot(a, b):
    return jnp.dot(a, b, precision=HIGHEST, preferred_element_type=F32)


def split(value):
    high = value.astype(BF16)
    return high, (value - high.astype(F32)).astype(BF16)


def bdot(a, b):
    return jnp.dot(a, b, preferred_element_type=F32)


def eliminate(blocks, first, last):
    index = lax.broadcasted_iota(jnp.int32, (8, 1), 0)
    for j in range(first, last, GROUP):
        own, at = j // 8, j % 8
        steps = range(GROUP)
        columns = {
            (k, t): jnp.broadcast_to(blocks[k][:, j + t : j + t + 1], (8, 2 * RANK))
            for k in range(own, RANK // 8) for t in steps
        }
        rows = [blocks[own][at + t : at + t + 1, :] for t in steps]
        small = {(i, t): columns[own, t][at + i : at + i + 1, :] for i in steps for t in steps}
        unit, ratio = [], {}
        for t in steps:
            inverse = 1.0 / small[t, t]
            unit.append(rows[t] * inverse)
            for i in range(t + 1, GROUP):
                ratio[t, i] = small[t, i] * inverse
            for i in range(t + 1, GROUP):
                rows[i] = rows[i] - small[i, t] * unit[t]
                for k in range(t + 1, GROUP):
                    small[i, k] = small[i, k] - small[i, t] * ratio[t, k]
        for k in range(own, RANK // 8):
            value, done = blocks[k], []
            for t in steps:
                column = columns[k, t]
                for i in range(t):
                    column = column - done[i] * ratio[i, t]
                done.append(column)
                value = value - column * unit[t]
            if k == own:
                value = jnp.where(index >= at + GROUP, value, blocks[k])
                for t in steps:
                    value = jnp.where(index == at + t, rows[t], value)
            blocks[k] = value
    return blocks


def step_kernel(
    delta, error, basis_t, weights, momentum, anchor,
    new_weights, new_momentum, new_anchor, new_error, new_basis,
    d_buf, e_buf, b_buf, w_buf, m_buf, a_buf, merged, total, coef, msib, mst, lbuf, l96, term, ra1, rc1, ra2, rc2, gfull, gy, gz, gx,
    load_sem, late_sem, sib_sem, left_sem, sem1, sem2, sem3, fwd_sem, gram_sem,
):
    x = lax.axis_index("group")
    shard = lax.axis_index("shard")
    z = lax.div(shard, 8)
    y = lax.rem(lax.div(shard, 2), 4)
    c = lax.rem(shard, 2)
    plane = x * NY + y

    xs = [lax.rem(x + d, NX) for d in range(NX)]
    ys = [lax.rem(y + d, NY) for d in range(NY)]
    zs = [lax.rem(z + d, NZ) for d in range(NZ)]
    cs = [c, 1 - c]
    known = {}

    def device(dx, dy, dz, dc):
        key = (dx, dy, dz, dc)
        if key not in known:
            known[key] = (xs[dx], zs[dz] * 8 + ys[dy] * 2 + cs[dc])
        return known[key]

    sibling = device(0, 0, 0, 1)

    barrier = pltpu.get_barrier_semaphore()
    peers = [device(0, 0, d, 0) for d in ZORDER]
    peers += [device(dx, dy, 0, 0) for dx, dy in XYORDER]
    peers += [device(dx, 0, 0, 1) for dx in (2, 1, 3, 0)]
    for peer in peers:
        pl.semaphore_signal(barrier, inc=1, device_id=peer, device_id_type=MESH)

    columns = [hint(((1 - c) * HALF + k * LOAD) % D, 128) for k in range(D // LOAD)]
    loads = []
    for k, col in enumerate(columns):
        cols = pl.ds(col, LOAD)
        group = []
        for j, (src, dst) in enumerate(((delta, d_buf), (error, e_buf), (basis_t, b_buf))):
            copy = pltpu.make_async_copy(src.at[:, cols], dst.at[:, cols], load_sem.at[k, j])
            copy.start()
            group.append(copy)
        loads.append(group)

    late = []
    for j, (src, dst) in enumerate(((weights, w_buf), (momentum, m_buf), (anchor, a_buf))):
        copy = pltpu.make_async_copy(src, dst, late_sem.at[j])
        copy.start()
        late.append(copy)

    pending = []

    def link(src, dst, sems, n, peer):
        return pltpu.make_async_remote_copy(
            src_ref=src, dst_ref=dst, send_sem=sems.at[0, n], recv_sem=sems.at[1, n],
            device_id=peer, device_id_type=MESH,
        )

    def send_all(pieces, sems, n, like):
        for src, dst, peer in pieces:
            link(src, dst, sems, n, peer).start()
        copy = link(like, like, sems, n, sibling)
        pending.append(copy)
        return copy

    mine = pl.ds(hint(c * ROWS, 16), ROWS)
    mine_low = pl.ds(hint((2 + c) * ROWS, 16), ROWS)
    theirs = pl.ds(hint((1 - c) * ROWS, 16), ROWS)
    theirs_low = pl.ds(hint((3 - c) * ROWS, 16), ROWS)
    part = jnp.zeros((2 * ROWS, 2 * RANK), F32)
    for k, col in enumerate(columns):
        for copy in loads[k]:
            copy.wait()
        cols = pl.ds(col, LOAD)
        value = d_buf[:, cols] + e_buf[:, cols]
        merged[:, cols] = value
        high, low = split(value)
        if k >= 2:
            mst[mine, (k - 2) * LOAD : (k - 1) * LOAD] = high
            mst[mine_low, (k - 2) * LOAD : (k - 1) * LOAD] = low
        part = part + lax.dot_general(
            jnp.concatenate([high, low], axis=0), jnp.concatenate(split(b_buf[:, cols]), axis=0),
            (((1,), (1,)), ((), ())), preferred_element_type=F32,
        )
    pl.semaphore_wait(barrier, len(peers))
    part = part[:ROWS] + part[ROWS:]
    part = part + pltpu.roll(part, RANK, 1)
    low_lanes = lax.broadcasted_iota(jnp.int32, (ROWS // 2, 2 * RANK), 1) < RANK
    lbuf[c * NX + x] = jnp.where(low_lanes, part[: ROWS // 2], part[ROWS // 2 :])

    slot = lbuf.at[c * NX + x]
    lefts = send_all([(slot, slot, device(dx, 0, 0, dc)) for dx, dc in PLANEORDER], left_sem, 0, lbuf.at[0:7])
    away = merged.at[:, pl.ds(hint((1 - c) * HALF, 128), HALF)]
    moved = send_all([(away, msib, sibling)], sib_sem, 0, msib)
    moved.wait_recv()
    mst[theirs, :], mst[theirs_low, :] = split(msib[...])
    lefts.wait_recv()
    for core in range(2):
        packed = ((lbuf[core * NX] + lbuf[core * NX + 1]) + lbuf[core * NX + 2]) + lbuf[core * NX + 3]
        l96[core * ROWS : core * ROWS + ROWS // 2, :] = jnp.where(low_lanes, packed, 0.0)
        l96[core * ROWS + ROWS // 2 : (core + 1) * ROWS, :] = jnp.where(low_lanes, pltpu.roll(packed, RANK, 1), 0.0)
    left = l96[...]
    left_high = left.astype(BF16).astype(F32)
    pair = left_high + pltpu.roll(left - left_high, RANK, 1)
    left_t = jnp.transpose(jnp.concatenate([pair, pair], axis=0)).astype(BF16)

    def terms(start, width):
        value = bdot(left_t, mst[:, start : start + width])
        term[:, start : start + width] = value[:RANK] + value[RANK:]

    count = len(CHUNKS)
    z_rows = pl.ds(hint(z * 8, 8), 8)
    plane_rows = pl.ds(hint(lax.div(plane, 2) * 8, 8), 8)
    plane_col = lax.rem(plane, 2) * PLANE
    out_rows = [pl.ds(hint(zs[d] * 8, 8), 8) for d in range(NZ)]
    out_plane = {}
    for dx, dy in XYORDER:
        piece = xs[dx] * NY + ys[dy]
        out_plane[dx, dy] = (pl.ds(hint(lax.div(piece, 2) * 8, 8), 8), lax.rem(piece, 2) * PLANE)

    def over_z(src, dst, sems, n, like):
        return send_all([(src, dst, device(0, 0, d, 0)) for d in ZORDER], sems, n, like)

    def over_xy(src, dst, sems, n, like):
        return send_all([(src, dst, device(dx, dy, 0, 0)) for dx, dy in XYORDER], sems, n, like)

    def stage0(n):
        zfirst, off, width = CHUNKS[n]
        cols = pl.ds(off, width)
        if zfirst:
            start = 2 * PLANE + off
            terms(start, width)
            pieces = [(term.at[out_rows[d], pl.ds(start, width)], rc1.at[d, :, cols], device(0, 0, d, 0)) for d in ZORDER]
            return send_all(pieces, sem1, n, rc1.at[1:NZ, :, cols])
        for side in range(2):
            terms(side * PLANE + off, width)
        pieces = []
        for dx, dy in XYORDER:
            rows, col = out_plane[dx, dy]
            src = term.at[rows, pl.ds(hint(col + off, 128), width)]
            pieces.append((src, ra1.at[dx * NY + dy, :, cols], device(dx, dy, 0, 0)))
        return send_all(pieces, sem1, n, ra1.at[1 : NX * NY, :, cols])

    def stage1(n):
        zfirst, off, width = CHUNKS[n]
        cols = pl.ds(off, width)
        first[n].wait_recv()
        if zfirst:
            value = term[z_rows, pl.ds(2 * PLANE + off, width)]
            for d in range(1, NZ):
                value = value + rc1[d, :, cols]
            rc2[plane, :, cols] = value
            piece = rc2.at[plane, :, cols]
            return over_xy(piece, piece, sem2, n, rc2.at[1 : NX * NY, :, cols])
        value = term[plane_rows, pl.ds(hint(plane_col + off, 128), width)]
        for d in range(1, NX * NY):
            value = value + ra1[d, :, cols]
        ra2[z, :, cols] = value
        piece = ra2.at[z, :, cols]
        return over_z(piece, piece, sem2, n, ra2.at[1:NZ, :, cols])

    def stage2(n):
        zfirst, off, width = CHUNKS[n]
        cols = pl.ds(off, width)
        second[n].wait_recv()
        if zfirst:
            value = rc2[0, :, cols]
            for k in range(1, NX * NY):
                value = value + rc2[k, :, cols]
            place = (z_rows, pl.ds(hint(c * HALF + 2 * PLANE + off, 128), width))
            total[place] = value
            return over_z(total.at[place], total.at[place], sem3, n, rc1.at[1:NZ, :, cols])
        value = ra2[0, :, cols]
        for k in range(1, NZ):
            value = value + ra2[k, :, cols]
        place = (plane_rows, pl.ds(hint(c * HALF + plane_col + off, 128), width))
        total[place] = value
        return over_xy(total.at[place], total.at[place], sem3, n, ra1.at[1 : NX * NY, :, cols])

    def ranges(n, core):
        zfirst, off, width = CHUNKS[n]
        starts = (2 * PLANE + off,) if zfirst else (off, PLANE + off)
        return [pl.ds(hint(core * HALF + start, 128), width) for start in starts]

    def stage3(n):
        third[n].wait_recv()
        places = [total.at[:, cols] for cols in ranges(n, c)]
        return send_all([(p, p, sibling) for p in places], fwd_sem, n, term.at[:, 0 : len(places) * CHUNKS[n][2]])

    share = x * 2 + c

    def gram_start():
        gfull[...] = dot(jnp.transpose(left)[:RANK], left)
        gy[y] = gfull[pl.ds(hint(share * 8, 8), 8), :]
        pieces = [(gy.at[y], gy.at[y], device(0, d, 0, 0)) for d in (2, 1, 3)]
        return send_all(pieces, gram_sem, 0, gy.at[1:NY])

    def gram_middle(copies):
        copies.wait_recv()
        gz[z] = ((gy[0] + gy[1]) + gy[2]) + gy[3]
        return over_z(gz.at[z], gz.at[z], gram_sem, 1, gz.at[1:NZ])

    def gram_end(copies):
        copies.wait_recv()
        value = gz[0]
        for k in range(1, NZ):
            value = value + gz[k]
        gx[share] = value
        pieces = [(gx.at[share], gx.at[share], device(dx, 0, 0, dc)) for dx, dc in PLANEORDER]
        return send_all(pieces, gram_sem, 2, gx.at[1:8])

    def gram_blocks():
        lane = lax.broadcasted_iota(jnp.int32, (8, 2 * RANK), 1)
        row = lax.broadcasted_iota(jnp.int32, (8, 2 * RANK), 0)
        return [
            jnp.where(lane < RANK, gx[k], jnp.where(lane == row + (RANK + 8 * k), 1.0, 0.0)) for k in range(RANK // 8)
        ]

    def coefficients(blocks):
        whole = jnp.concatenate(blocks, axis=0)
        lane = lax.broadcasted_iota(jnp.int32, (RANK, 2 * RANK), 1)
        row = lax.broadcasted_iota(jnp.int32, (RANK, 2 * RANK), 0)
        pivot = jnp.sum(jnp.where(lane == row, whole, 0.0), axis=1, keepdims=True)
        scale = lax.rsqrt(pivot)
        scale = scale * (1.5 - 0.5 * pivot * scale * scale)
        inverse = (pltpu.roll(whole, RANK, 1) * scale)[:, :RANK]
        own = l96[pl.ds(hint(c * ROWS, 8), ROWS), 0:RANK]
        ortho = dot_nt(own, inverse)
        both = 0.25 * jnp.concatenate([inverse, dot(ortho, inverse)], axis=0)
        high, low = split(both)
        coef[...] = jnp.concatenate([high, high, low, low], axis=1)

    def update(cols):
        high, low = split(total[:, cols])
        both = bdot(coef[...], jnp.concatenate([high, low, high, low], axis=0))
        new_basis[:, cols] = both[:RANK]
        approx = both[RANK:]
        new_error[:, cols] = merged[:, cols] - approx
        speed = nesterov_mu * m_buf[:, cols] + approx
        new_momentum[:, cols] = speed
        stepped = w_buf[:, cols] - outer_rate * (approx + nesterov_mu * speed)
        new_weights[:, cols] = stepped
        new_anchor[:, cols] = anchor_decay * a_buf[:, cols] + (1.0 - anchor_decay) * stepped

    def update_own(n):
        for cols in ranges(n, c):
            update(cols)

    def update_sibling(n):
        fourth[n].wait_recv()
        for cols in ranges(n, 1 - c):
            update(cols)

    early = count // 2
    first = [stage0(0)]
    gram = gram_start()
    first += [stage0(n) for n in range(1, count)]
    gram = gram_middle(gram)
    second = [stage1(n) for n in range(early)]
    gram = gram_end(gram)
    second += [stage1(n) for n in range(early, count)]
    third = [stage2(n) for n in range(early)]
    gram.wait_recv()
    blocks = eliminate(gram_blocks(), 0, 16)
    for n in range(early, count):
        third.append(stage2(n))
        if n < count - 1:
            blocks = eliminate(blocks, 16, 32)
    coefficients(eliminate(blocks, 32, RANK))
    for copy in late:
        copy.wait()
    fourth = []
    for n in range(count):
        fourth.append(stage3(n))
        if n:
            update_own(n - 1)
    for n in range(count - 1):
        update_sibling(n)
    update_own(count - 1)
    update_sibling(count - 1)
    for copy in pending:
        copy.wait_send()


def store_kernel(*refs):
    sems = refs[-1]
    count = len(refs) // 2
    copies = [pltpu.make_async_copy(refs[k], refs[count + k], sems.at[k]) for k in range(count)]
    for copy in copies:
        copy.start()
    for copy in copies:
        copy.wait()


def per_device(delta, error, weights, momentum, anchor, basis):
    count = len(CHUNKS)
    hbm = pl.BlockSpec(memory_space=pltpu.HBM)
    vmem = pl.BlockSpec(memory_space=pltpu.VMEM)
    dma = pltpu.SemaphoreType.DMA
    shapes = [jax.ShapeDtypeStruct((ROWS, D), F32)] * 4 + [jax.ShapeDtypeStruct((RANK, D), F32)]
    outs = pl.pallas_call(
        step_kernel,
        out_shape=shapes,
        in_specs=[hbm] * 6,
        out_specs=[vmem] * 5,
        scratch_shapes=[
            pltpu.VMEM((ROWS, D), F32),
            pltpu.VMEM((ROWS, D), F32),
            pltpu.VMEM((RANK, D), F32),
            pltpu.VMEM((ROWS, D), F32),
            pltpu.VMEM((ROWS, D), F32),
            pltpu.VMEM((ROWS, D), F32),
            pltpu.VMEM((ROWS, D), F32),
            pltpu.VMEM((RANK, D), F32),
            pltpu.VMEM((RANK + ROWS, 4 * RANK), BF16),
            pltpu.VMEM((ROWS, HALF), F32),
            pltpu.VMEM((4 * ROWS, HALF), BF16),
            pltpu.VMEM((2 * NX, ROWS // 2, 2 * RANK), F32),
            pltpu.VMEM((2 * ROWS, 2 * RANK), F32),
            pltpu.VMEM((RANK, HALF), F32),
            pltpu.VMEM((NX * NY, 8, PLANE), F32),
            pltpu.VMEM((NZ, 8, ZFIRST), F32),
            pltpu.VMEM((NZ, 8, PLANE), F32),
            pltpu.VMEM((NX * NY, 8, ZFIRST), F32),
            pltpu.VMEM((RANK, 2 * RANK), F32),
            pltpu.VMEM((NY, 8, 2 * RANK), F32),
            pltpu.VMEM((NZ, 8, 2 * RANK), F32),
            pltpu.VMEM((8, 8, 2 * RANK), F32),
            dma((D // LOAD, 3)),
            dma((3,)),
            dma((2, 1)),
            dma((2, 1)),
            dma((2, count)),
            dma((2, count)),
            dma((2, count)),
            dma((2, count)),
            dma((2, 3)),
        ],
        compiler_params=pltpu.CompilerParams(collective_id=0, has_side_effects=True, vmem_limit_bytes=32 << 20),
    )(*(pltpu.with_memory_space_constraint(a, pltpu.HBM) for a in (delta[0], error[0], basis.T, weights, momentum, anchor)))
    outs = pl.pallas_call(
        store_kernel,
        out_shape=shapes,
        in_specs=[vmem] * 5,
        out_specs=[hbm] * 5,
        scratch_shapes=[dma((5,))],
        compiler_params=pltpu.CompilerParams(vmem_limit_bytes=1 << 20),
    )(*(pltpu.with_memory_space_constraint(a, pltpu.VMEM) for a in outs))
    new_weights, new_momentum, new_anchor, new_error, new_basis = outs
    return (new_weights, new_momentum, new_anchor, new_error[None], new_basis.T)


def solution(mesh):
    in_specs = (
        P("group", "shard", None),
        P("group", "shard", None),
        P("shard", None),
        P("shard", None),
        P("shard", None),
        P(),
    )
    out_specs = (
        P("shard", None),
        P("shard", None),
        P("shard", None),
        P("group", "shard", None),
        P(),
    )
    return jax.shard_map(
        per_device, mesh=mesh, in_specs=in_specs, out_specs=out_specs, check_vma=False
    )
```

```python
import jax
import jax.numpy as jnp
from jax import lax
from jax.experimental import pallas as pl
from jax.experimental.pallas import tpu as pltpu
from jax.sharding import PartitionSpec as P

MESH = pl.DeviceIdType.MESH
HIGHEST = lax.Precision.HIGHEST
F32 = jnp.float32
BF16 = jnp.bfloat16

outer_rate = 0.7
nesterov_mu = 0.9
anchor_decay = 0.9

D = 5120
RANK = 64
ROWS = 48
NX, NY, NZ = 4, 4, 8
HALF = D // 2
PLANE = 896
ZFIRST = HALF - 2 * PLANE
CHUNKS = ((True, 0, 256), (False, 0, 384), (True, 256, 256), (False, 384, 256), (True, 512, 256), (False, 640, 256))
LOAD = 1280
GROUP = 4
ZORDER = (4, 3, 5, 2, 6, 1, 7)
PLANEORDER = ((2, 0), (2, 1), (1, 0), (3, 0), (1, 1), (3, 1), (0, 1))
XYORDER = ((2, 2), (2, 1), (2, 3), (1, 2), (3, 2), (2, 0), (0, 2), (1, 1), (1, 3), (3, 1), (3, 3), (1, 0), (3, 0), (0, 1), (0, 3))


def hint(value, multiple):
    return pl.multiple_of(value, multiple)


def dot_nt(a, b):
    return lax.dot_general(a, b, (((1,), (1,)), ((), ())), precision=HIGHEST, preferred_element_type=F32)


def dot(a, b):
    return jnp.dot(a, b, precision=HIGHEST, preferred_element_type=F32)


def split(value):
    high = value.astype(BF16)
    return high, (value - high.astype(F32)).astype(BF16)


def bdot(a, b):
    return jnp.dot(a, b, preferred_element_type=F32)


def eliminate(blocks, first, last):
    index = lax.broadcasted_iota(jnp.int32, (8, 1), 0)
    for j in range(first, last, GROUP):
        own, at = j // 8, j % 8
        steps = range(GROUP)
        columns = {
            (k, t): jnp.broadcast_to(blocks[k][:, j + t : j + t + 1], (8, 2 * RANK))
            for k in range(own, RANK // 8) for t in steps
        }
        rows = [blocks[own][at + t : at + t + 1, :] for t in steps]
        small = {(i, t): columns[own, t][at + i : at + i + 1, :] for i in steps for t in steps}
        unit, ratio = [], {}
        for t in steps:
            inverse = 1.0 / small[t, t]
            unit.append(rows[t] * inverse)
            for i in range(t + 1, GROUP):
                ratio[t, i] = small[t, i] * inverse
            for i in range(t + 1, GROUP):
                rows[i] = rows[i] - small[i, t] * unit[t]
                for k in range(t + 1, GROUP):
                    small[i, k] = small[i, k] - small[i, t] * ratio[t, k]
        for k in range(own, RANK // 8):
            value, done = blocks[k], []
            for t in steps:
                column = columns[k, t]
                for i in range(t):
                    column = column - done[i] * ratio[i, t]
                done.append(column)
                value = value - column * unit[t]
            if k == own:
                value = jnp.where(index >= at + GROUP, value, blocks[k])
                for t in steps:
                    value = jnp.where(index == at + t, rows[t], value)
            blocks[k] = value
    return blocks


def step_kernel(
    delta, error, basis_t, weights, momentum, anchor,
    new_weights, new_momentum, new_anchor, new_error, new_basis,
    d_buf, e_buf, b_buf, w_buf, m_buf, a_buf, merged, total, coef, msib, mst, lbuf, l96, term, ra1, rc1, ra2, rc2, gfull, gy, gz, gx,
    load_sem, late_sem, sib_sem, left_sem, sem1, sem2, sem3, fwd_sem, gram_sem,
):
    x = lax.axis_index("group")
    shard = lax.axis_index("shard")
    z = lax.div(shard, 8)
    y = lax.rem(lax.div(shard, 2), 4)
    c = lax.rem(shard, 2)
    plane = x * NY + y

    xs = [lax.rem(x + d, NX) for d in range(NX)]
    ys = [lax.rem(y + d, NY) for d in range(NY)]
    zs = [lax.rem(z + d, NZ) for d in range(NZ)]
    cs = [c, 1 - c]
    known = {}

    def device(dx, dy, dz, dc):
        key = (dx, dy, dz, dc)
        if key not in known:
            known[key] = (xs[dx], zs[dz] * 8 + ys[dy] * 2 + cs[dc])
        return known[key]

    sibling = device(0, 0, 0, 1)

    barrier = pltpu.get_barrier_semaphore()
    peers = [device(0, 0, d, 0) for d in ZORDER]
    peers += [device(dx, dy, 0, 0) for dx, dy in XYORDER]
    peers += [device(dx, 0, 0, 1) for dx in (2, 1, 3, 0)]
    for peer in peers:
        pl.semaphore_signal(barrier, inc=1, device_id=peer, device_id_type=MESH)

    columns = [hint(((1 - c) * HALF + k * LOAD) % D, 128) for k in range(D // LOAD)]
    loads = []
    for k, col in enumerate(columns):
        cols = pl.ds(col, LOAD)
        group = []
        for j, (src, dst) in enumerate(((delta, d_buf), (error, e_buf), (basis_t, b_buf))):
            copy = pltpu.make_async_copy(src.at[:, cols], dst.at[:, cols], load_sem.at[k, j])
            copy.start()
            group.append(copy)
        loads.append(group)

    late = []
    for j, (src, dst) in enumerate(((weights, w_buf), (momentum, m_buf), (anchor, a_buf))):
        copy = pltpu.make_async_copy(src, dst, late_sem.at[j])
        copy.start()
        late.append(copy)

    pending = []

    def link(src, dst, sems, n, peer):
        return pltpu.make_async_remote_copy(
            src_ref=src, dst_ref=dst, send_sem=sems.at[0, n], recv_sem=sems.at[1, n],
            device_id=peer, device_id_type=MESH,
        )

    def send_all(pieces, sems, n, like):
        for src, dst, peer in pieces:
            link(src, dst, sems, n, peer).start()
        copy = link(like, like, sems, n, sibling)
        pending.append(copy)
        return copy

    mine = pl.ds(hint(c * ROWS, 16), ROWS)
    mine_low = pl.ds(hint((2 + c) * ROWS, 16), ROWS)
    theirs = pl.ds(hint((1 - c) * ROWS, 16), ROWS)
    theirs_low = pl.ds(hint((3 - c) * ROWS, 16), ROWS)
    part = jnp.zeros((2 * ROWS, 2 * RANK), F32)
    for k, col in enumerate(columns):
        for copy in loads[k]:
            copy.wait()
        cols = pl.ds(col, LOAD)
        value = d_buf[:, cols] + e_buf[:, cols]
        merged[:, cols] = value
        high, low = split(value)
        if k >= 2:
            mst[mine, (k - 2) * LOAD : (k - 1) * LOAD] = high
            mst[mine_low, (k - 2) * LOAD : (k - 1) * LOAD] = low
        part = part + lax.dot_general(
            jnp.concatenate([high, low], axis=0), jnp.concatenate(split(b_buf[:, cols]), axis=0),
            (((1,), (1,)), ((), ())), preferred_element_type=F32,
        )
    part = part[:ROWS] + part[ROWS:]
    part = part + pltpu.roll(part, RANK, 1)
    low_lanes = lax.broadcasted_iota(jnp.int32, (ROWS // 2, 2 * RANK), 1) < RANK
    lbuf[c * NX + x] = jnp.where(low_lanes, part[: ROWS // 2], part[ROWS // 2 :])

    pl.semaphore_wait(barrier, len(peers))
    slot = lbuf.at[c * NX + x]
    lefts = send_all([(slot, slot, device(dx, 0, 0, dc)) for dx, dc in PLANEORDER], left_sem, 0, lbuf.at[0:7])
    away = merged.at[:, pl.ds(hint((1 - c) * HALF, 128), HALF)]
    moved = send_all([(away, msib, sibling)], sib_sem, 0, msib)
    moved.wait_recv()
    mst[theirs, :], mst[theirs_low, :] = split(msib[...])
    lefts.wait_recv()
    for core in range(2):
        packed = ((lbuf[core * NX] + lbuf[core * NX + 1]) + lbuf[core * NX + 2]) + lbuf[core * NX + 3]
        l96[core * ROWS : core * ROWS + ROWS // 2, :] = jnp.where(low_lanes, packed, 0.0)
        l96[core * ROWS + ROWS // 2 : (core + 1) * ROWS, :] = jnp.where(low_lanes, pltpu.roll(packed, RANK, 1), 0.0)
    left = l96[...]
    left_high = left.astype(BF16).astype(F32)
    pair = left_high + pltpu.roll(left - left_high, RANK, 1)
    left_t = jnp.transpose(jnp.concatenate([pair, pair], axis=0)).astype(BF16)

    def terms(start, width):
        value = bdot(left_t, mst[:, start : start + width])
        term[:, start : start + width] = value[:RANK] + value[RANK:]

    count = len(CHUNKS)
    z_rows = pl.ds(hint(z * 8, 8), 8)
    plane_rows = pl.ds(hint(lax.div(plane, 2) * 8, 8), 8)
    plane_col = lax.rem(plane, 2) * PLANE
    out_rows = [pl.ds(hint(zs[d] * 8, 8), 8) for d in range(NZ)]
    out_plane = {}
    for dx, dy in XYORDER:
        piece = xs[dx] * NY + ys[dy]
        out_plane[dx, dy] = (pl.ds(hint(lax.div(piece, 2) * 8, 8), 8), lax.rem(piece, 2) * PLANE)

    def over_z(src, dst, sems, n, like):
        return send_all([(src, dst, device(0, 0, d, 0)) for d in ZORDER], sems, n, like)

    def over_xy(src, dst, sems, n, like):
        return send_all([(src, dst, device(dx, dy, 0, 0)) for dx, dy in XYORDER], sems, n, like)

    def stage0(n):
        zfirst, off, width = CHUNKS[n]
        cols = pl.ds(off, width)
        if zfirst:
            start = 2 * PLANE + off
            terms(start, width)
            pieces = [(term.at[out_rows[d], pl.ds(start, width)], rc1.at[d, :, cols], device(0, 0, d, 0)) for d in ZORDER]
            return send_all(pieces, sem1, n, rc1.at[1:NZ, :, cols])
        for side in range(2):
            terms(side * PLANE + off, width)
        pieces = []
        for dx, dy in XYORDER:
            rows, col = out_plane[dx, dy]
            src = term.at[rows, pl.ds(hint(col + off, 128), width)]
            pieces.append((src, ra1.at[dx * NY + dy, :, cols], device(dx, dy, 0, 0)))
        return send_all(pieces, sem1, n, ra1.at[1 : NX * NY, :, cols])

    def stage1(n):
        zfirst, off, width = CHUNKS[n]
        cols = pl.ds(off, width)
        first[n].wait_recv()
        if zfirst:
            value = term[z_rows, pl.ds(2 * PLANE + off, width)]
            for d in range(1, NZ):
                value = value + rc1[d, :, cols]
            rc2[plane, :, cols] = value
            piece = rc2.at[plane, :, cols]
            return over_xy(piece, piece, sem2, n, rc2.at[1 : NX * NY, :, cols])
        value = term[plane_rows, pl.ds(hint(plane_col + off, 128), width)]
        for d in range(1, NX * NY):
            value = value + ra1[d, :, cols]
        ra2[z, :, cols] = value
        piece = ra2.at[z, :, cols]
        return over_z(piece, piece, sem2, n, ra2.at[1:NZ, :, cols])

    def stage2(n):
        zfirst, off, width = CHUNKS[n]
        cols = pl.ds(off, width)
        second[n].wait_recv()
        if zfirst:
            value = rc2[0, :, cols]
            for k in range(1, NX * NY):
                value = value + rc2[k, :, cols]
            place = (z_rows, pl.ds(hint(c * HALF + 2 * PLANE + off, 128), width))
            total[place] = value
            return over_z(total.at[place], total.at[place], sem3, n, rc1.at[1:NZ, :, cols])
        value = ra2[0, :, cols]
        for k in range(1, NZ):
            value = value + ra2[k, :, cols]
        place = (plane_rows, pl.ds(hint(c * HALF + plane_col + off, 128), width))
        total[place] = value
        return over_xy(total.at[place], total.at[place], sem3, n, ra1.at[1 : NX * NY, :, cols])

    def ranges(n, core):
        zfirst, off, width = CHUNKS[n]
        starts = (2 * PLANE + off,) if zfirst else (off, PLANE + off)
        return [pl.ds(hint(core * HALF + start, 128), width) for start in starts]

    def stage3(n):
        third[n].wait_recv()
        places = [total.at[:, cols] for cols in ranges(n, c)]
        return send_all([(p, p, sibling) for p in places], fwd_sem, n, term.at[:, 0 : len(places) * CHUNKS[n][2]])

    share = x * 2 + c

    def gram_start():
        gfull[...] = dot(jnp.transpose(left)[:RANK], left)
        gy[y] = gfull[pl.ds(hint(share * 8, 8), 8), :]
        pieces = [(gy.at[y], gy.at[y], device(0, d, 0, 0)) for d in (2, 1, 3)]
        return send_all(pieces, gram_sem, 0, gy.at[1:NY])

    def gram_middle(copies):
        copies.wait_recv()
        gz[z] = ((gy[0] + gy[1]) + gy[2]) + gy[3]
        return over_z(gz.at[z], gz.at[z], gram_sem, 1, gz.at[1:NZ])

    def gram_end(copies):
        copies.wait_recv()
        value = gz[0]
        for k in range(1, NZ):
            value = value + gz[k]
        gx[share] = value
        pieces = [(gx.at[share], gx.at[share], device(dx, 0, 0, dc)) for dx, dc in PLANEORDER]
        return send_all(pieces, gram_sem, 2, gx.at[1:8])

    def gram_blocks():
        lane = lax.broadcasted_iota(jnp.int32, (8, 2 * RANK), 1)
        row = lax.broadcasted_iota(jnp.int32, (8, 2 * RANK), 0)
        return [
            jnp.where(lane < RANK, gx[k], jnp.where(lane == row + (RANK + 8 * k), 1.0, 0.0)) for k in range(RANK // 8)
        ]

    def coefficients(blocks):
        whole = jnp.concatenate(blocks, axis=0)
        lane = lax.broadcasted_iota(jnp.int32, (RANK, 2 * RANK), 1)
        row = lax.broadcasted_iota(jnp.int32, (RANK, 2 * RANK), 0)
        pivot = jnp.sum(jnp.where(lane == row, whole, 0.0), axis=1, keepdims=True)
        scale = lax.rsqrt(pivot)
        scale = scale * (1.5 - 0.5 * pivot * scale * scale)
        inverse = (pltpu.roll(whole, RANK, 1) * scale)[:, :RANK]
        own = l96[pl.ds(hint(c * ROWS, 8), ROWS), 0:RANK]
        ortho = dot_nt(own, inverse)
        both = 0.25 * jnp.concatenate([inverse, dot(ortho, inverse)], axis=0)
        high, low = split(both)
        coef[...] = jnp.concatenate([high, high, low, low], axis=1)

    def update(cols):
        high, low = split(total[:, cols])
        both = bdot(coef[...], jnp.concatenate([high, low, high, low], axis=0))
        new_basis[:, cols] = both[:RANK]
        approx = both[RANK:]
        new_error[:, cols] = merged[:, cols] - approx
        speed = nesterov_mu * m_buf[:, cols] + approx
        new_momentum[:, cols] = speed
        stepped = w_buf[:, cols] - outer_rate * (approx + nesterov_mu * speed)
        new_weights[:, cols] = stepped
        new_anchor[:, cols] = anchor_decay * a_buf[:, cols] + (1.0 - anchor_decay) * stepped

    def update_own(n):
        for cols in ranges(n, c):
            update(cols)

    def update_sibling(n):
        fourth[n].wait_recv()
        for cols in ranges(n, 1 - c):
            update(cols)

    early = count // 2
    gram = gram_start()
    first = [stage0(n) for n in range(count)]
    gram = gram_middle(gram)
    second = [stage1(n) for n in range(count)]
    gram = gram_end(gram)
    third = [stage2(n) for n in range(count)]
    gram.wait_recv()
    coefficients(eliminate(gram_blocks(), 0, RANK))
    for copy in late:
        copy.wait()
    fourth = []
    for n in range(count):
        fourth.append(stage3(n))
        if n:
            update_own(n - 1)
    for n in range(count - 1):
        update_sibling(n)
    update_own(count - 1)
    update_sibling(count - 1)
    for copy in pending:
        copy.wait_send()


def store_kernel(*refs):
    sems = refs[-1]
    count = len(refs) // 2
    copies = [pltpu.make_async_copy(refs[k], refs[count + k], sems.at[k]) for k in range(count)]
    for copy in copies:
        copy.start()
    for copy in copies:
        copy.wait()


def per_device(delta, error, weights, momentum, anchor, basis):
    count = len(CHUNKS)
    hbm = pl.BlockSpec(memory_space=pltpu.HBM)
    vmem = pl.BlockSpec(memory_space=pltpu.VMEM)
    dma = pltpu.SemaphoreType.DMA
    shapes = [jax.ShapeDtypeStruct((ROWS, D), F32)] * 4 + [jax.ShapeDtypeStruct((RANK, D), F32)]
    outs = pl.pallas_call(
        step_kernel,
        out_shape=shapes,
        in_specs=[hbm] * 6,
        out_specs=[vmem] * 5,
        scratch_shapes=[
            pltpu.VMEM((ROWS, D), F32),
            pltpu.VMEM((ROWS, D), F32),
            pltpu.VMEM((RANK, D), F32),
            pltpu.VMEM((ROWS, D), F32),
            pltpu.VMEM((ROWS, D), F32),
            pltpu.VMEM((ROWS, D), F32),
            pltpu.VMEM((ROWS, D), F32),
            pltpu.VMEM((RANK, D), F32),
            pltpu.VMEM((RANK + ROWS, 4 * RANK), BF16),
            pltpu.VMEM((ROWS, HALF), F32),
            pltpu.VMEM((4 * ROWS, HALF), BF16),
            pltpu.VMEM((2 * NX, ROWS // 2, 2 * RANK), F32),
            pltpu.VMEM((2 * ROWS, 2 * RANK), F32),
            pltpu.VMEM((RANK, HALF), F32),
            pltpu.VMEM((NX * NY, 8, PLANE), F32),
            pltpu.VMEM((NZ, 8, ZFIRST), F32),
            pltpu.VMEM((NZ, 8, PLANE), F32),
            pltpu.VMEM((NX * NY, 8, ZFIRST), F32),
            pltpu.VMEM((RANK, 2 * RANK), F32),
            pltpu.VMEM((NY, 8, 2 * RANK), F32),
            pltpu.VMEM((NZ, 8, 2 * RANK), F32),
            pltpu.VMEM((8, 8, 2 * RANK), F32),
            dma((D // LOAD, 3)),
            dma((3,)),
            dma((2, 1)),
            dma((2, 1)),
            dma((2, count)),
            dma((2, count)),
            dma((2, count)),
            dma((2, count)),
            dma((2, 3)),
        ],
        compiler_params=pltpu.CompilerParams(collective_id=0, has_side_effects=True, vmem_limit_bytes=32 << 20),
    )(*(pltpu.with_memory_space_constraint(a, pltpu.HBM) for a in (delta[0], error[0], basis.T, weights, momentum, anchor)))
    outs = pl.pallas_call(
        store_kernel,
        out_shape=shapes,
        in_specs=[vmem] * 5,
        out_specs=[hbm] * 5,
        scratch_shapes=[dma((5,))],
        compiler_params=pltpu.CompilerParams(vmem_limit_bytes=1 << 20),
    )(*(pltpu.with_memory_space_constraint(a, pltpu.VMEM) for a in outs))
    new_weights, new_momentum, new_anchor, new_error, new_basis = outs
    return (new_weights, new_momentum, new_anchor, new_error[None], new_basis.T)


def solution(mesh):
    in_specs = (
        P("group", "shard", None),
        P("group", "shard", None),
        P("shard", None),
        P("shard", None),
        P("shard", None),
        P(),
    )
    out_specs = (
        P("shard", None),
        P("shard", None),
        P("shard", None),
        P("group", "shard", None),
        P(),
    )
    return jax.shard_map(
        per_device, mesh=mesh, in_specs=in_specs, out_specs=out_specs, check_vma=False
    )
```

```python
import jax
import jax.numpy as jnp
from jax import lax
from jax.experimental import pallas as pl
from jax.experimental.pallas import tpu as pltpu
from jax.sharding import PartitionSpec as P

MESH = pl.DeviceIdType.MESH
HIGHEST = lax.Precision.HIGHEST
F32 = jnp.float32
BF16 = jnp.bfloat16

outer_rate = 0.7
nesterov_mu = 0.9
anchor_decay = 0.9

D = 5120
RANK = 64
ROWS = 48
NX, NY, NZ = 4, 4, 8
HALF = D // 2
PLANE = 896
ZFIRST = HALF - 2 * PLANE
CHUNKS = ((True, 0, 256), (False, 0, 256), (True, 256, 256), (False, 256, 256), (True, 512, 256), (False, 512, 256), (False, 768, 128))
LOAD = 1280
GROUP = 4
ZORDER = (4, 3, 5, 2, 6, 1, 7)
PLANEORDER = ((2, 0), (2, 1), (1, 0), (3, 0), (1, 1), (3, 1), (0, 1))
XYORDER = ((2, 2), (2, 1), (2, 3), (1, 2), (3, 2), (2, 0), (0, 2), (1, 1), (1, 3), (3, 1), (3, 3), (1, 0), (3, 0), (0, 1), (0, 3))


def hint(value, multiple):
    return pl.multiple_of(value, multiple)


def dot_nt(a, b):
    return lax.dot_general(a, b, (((1,), (1,)), ((), ())), precision=HIGHEST, preferred_element_type=F32)


def dot(a, b):
    return jnp.dot(a, b, precision=HIGHEST, preferred_element_type=F32)


def split(value):
    high = value.astype(BF16)
    return high, (value - high.astype(F32)).astype(BF16)


def bdot(a, b):
    return jnp.dot(a, b, preferred_element_type=F32)


def eliminate(blocks, first, last):
    index = lax.broadcasted_iota(jnp.int32, (8, 1), 0)
    for j in range(first, last, GROUP):
        own, at = j // 8, j % 8
        steps = range(GROUP)
        columns = {
            (k, t): jnp.broadcast_to(blocks[k][:, j + t : j + t + 1], (8, 2 * RANK))
            for k in range(own, RANK // 8) for t in steps
        }
        rows = [blocks[own][at + t : at + t + 1, :] for t in steps]
        small = {(i, t): columns[own, t][at + i : at + i + 1, :] for i in steps for t in steps}
        unit, ratio = [], {}
        for t in steps:
            inverse = 1.0 / small[t, t]
            unit.append(rows[t] * inverse)
            for i in range(t + 1, GROUP):
                ratio[t, i] = small[t, i] * inverse
            for i in range(t + 1, GROUP):
                rows[i] = rows[i] - small[i, t] * unit[t]
                for k in range(t + 1, GROUP):
                    small[i, k] = small[i, k] - small[i, t] * ratio[t, k]
        for k in range(own, RANK // 8):
            value, done = blocks[k], []
            for t in steps:
                column = columns[k, t]
                for i in range(t):
                    column = column - done[i] * ratio[i, t]
                done.append(column)
                value = value - column * unit[t]
            if k == own:
                value = jnp.where(index >= at + GROUP, value, blocks[k])
                for t in steps:
                    value = jnp.where(index == at + t, rows[t], value)
            blocks[k] = value
    return blocks


def step_kernel(
    delta, error, basis_t, weights, momentum, anchor,
    new_weights, new_momentum, new_anchor, new_error, new_basis,
    d_buf, e_buf, b_buf, w_buf, m_buf, a_buf, merged, total, coef, msib, mst, lbuf, l96, term, ra1, rc1, ra2, rc2, gfull, gy, gz, gx,
    load_sem, late_sem, sib_sem, left_sem, sem1, sem2, sem3, fwd_sem, gram_sem,
):
    x = lax.axis_index("group")
    shard = lax.axis_index("shard")
    z = lax.div(shard, 8)
    y = lax.rem(lax.div(shard, 2), 4)
    c = lax.rem(shard, 2)
    plane = x * NY + y

    xs = [lax.rem(x + d, NX) for d in range(NX)]
    ys = [lax.rem(y + d, NY) for d in range(NY)]
    zs = [lax.rem(z + d, NZ) for d in range(NZ)]
    cs = [c, 1 - c]
    known = {}

    def device(dx, dy, dz, dc):
        key = (dx, dy, dz, dc)
        if key not in known:
            known[key] = (xs[dx], zs[dz] * 8 + ys[dy] * 2 + cs[dc])
        return known[key]

    sibling = device(0, 0, 0, 1)

    barrier = pltpu.get_barrier_semaphore()
    peers = [device(0, 0, d, 0) for d in ZORDER]
    peers += [device(dx, dy, 0, 0) for dx, dy in XYORDER]
    peers += [device(dx, 0, 0, 1) for dx in (2, 1, 3, 0)]
    for peer in peers:
        pl.semaphore_signal(barrier, inc=1, device_id=peer, device_id_type=MESH)

    columns = [hint(((1 - c) * HALF + k * LOAD) % D, 128) for k in range(D // LOAD)]
    loads = []
    for k, col in enumerate(columns):
        cols = pl.ds(col, LOAD)
        group = []
        for j, (src, dst) in enumerate(((delta, d_buf), (error, e_buf), (basis_t, b_buf))):
            copy = pltpu.make_async_copy(src.at[:, cols], dst.at[:, cols], load_sem.at[k, j])
            copy.start()
            group.append(copy)
        loads.append(group)

    late = []
    for j, (src, dst) in enumerate(((weights, w_buf), (momentum, m_buf), (anchor, a_buf))):
        copy = pltpu.make_async_copy(src, dst, late_sem.at[j])
        copy.start()
        late.append(copy)

    pending = []

    def link(src, dst, sems, n, peer):
        return pltpu.make_async_remote_copy(
            src_ref=src, dst_ref=dst, send_sem=sems.at[0, n], recv_sem=sems.at[1, n],
            device_id=peer, device_id_type=MESH,
        )

    def send_all(pieces, sems, n, like):
        for src, dst, peer in pieces:
            link(src, dst, sems, n, peer).start()
        copy = link(like, like, sems, n, sibling)
        pending.append(copy)
        return copy

    mine = pl.ds(hint(c * ROWS, 16), ROWS)
    mine_low = pl.ds(hint((2 + c) * ROWS, 16), ROWS)
    theirs = pl.ds(hint((1 - c) * ROWS, 16), ROWS)
    theirs_low = pl.ds(hint((3 - c) * ROWS, 16), ROWS)
    part = jnp.zeros((2 * ROWS, 2 * RANK), F32)
    for k, col in enumerate(columns):
        for copy in loads[k]:
            copy.wait()
        cols = pl.ds(col, LOAD)
        value = d_buf[:, cols] + e_buf[:, cols]
        merged[:, cols] = value
        high, low = split(value)
        if k >= 2:
            mst[mine, (k - 2) * LOAD : (k - 1) * LOAD] = high
            mst[mine_low, (k - 2) * LOAD : (k - 1) * LOAD] = low
        part = part + lax.dot_general(
            jnp.concatenate([high, low], axis=0), jnp.concatenate(split(b_buf[:, cols]), axis=0),
            (((1,), (1,)), ((), ())), preferred_element_type=F32,
        )
    part = part[:ROWS] + part[ROWS:]
    part = part + pltpu.roll(part, RANK, 1)
    low_lanes = lax.broadcasted_iota(jnp.int32, (ROWS // 2, 2 * RANK), 1) < RANK
    lbuf[c * NX + x] = jnp.where(low_lanes, part[: ROWS // 2], part[ROWS // 2 :])

    pl.semaphore_wait(barrier, len(peers))
    slot = lbuf.at[c * NX + x]
    lefts = send_all([(slot, slot, device(dx, 0, 0, dc)) for dx, dc in PLANEORDER], left_sem, 0, lbuf.at[0:7])
    away = merged.at[:, pl.ds(hint((1 - c) * HALF, 128), HALF)]
    moved = send_all([(away, msib, sibling)], sib_sem, 0, msib)
    moved.wait_recv()
    mst[theirs, :], mst[theirs_low, :] = split(msib[...])
    lefts.wait_recv()
    for core in range(2):
        packed = ((lbuf[core * NX] + lbuf[core * NX + 1]) + lbuf[core * NX + 2]) + lbuf[core * NX + 3]
        l96[core * ROWS : core * ROWS + ROWS // 2, :] = jnp.where(low_lanes, packed, 0.0)
        l96[core * ROWS + ROWS // 2 : (core + 1) * ROWS, :] = jnp.where(low_lanes, pltpu.roll(packed, RANK, 1), 0.0)
    left = l96[...]
    left_high = left.astype(BF16).astype(F32)
    pair = left_high + pltpu.roll(left - left_high, RANK, 1)
    left_t = jnp.transpose(jnp.concatenate([pair, pair], axis=0)).astype(BF16)

    def terms(start, width):
        value = bdot(left_t, mst[:, start : start + width])
        term[:, start : start + width] = value[:RANK] + value[RANK:]

    count = len(CHUNKS)
    z_rows = pl.ds(hint(z * 8, 8), 8)
    plane_rows = pl.ds(hint(lax.div(plane, 2) * 8, 8), 8)
    plane_col = lax.rem(plane, 2) * PLANE
    out_rows = [pl.ds(hint(zs[d] * 8, 8), 8) for d in range(NZ)]
    out_plane = {}
    for dx, dy in XYORDER:
        piece = xs[dx] * NY + ys[dy]
        out_plane[dx, dy] = (pl.ds(hint(lax.div(piece, 2) * 8, 8), 8), lax.rem(piece, 2) * PLANE)

    def over_z(src, dst, sems, n, like):
        return send_all([(src, dst, device(0, 0, d, 0)) for d in ZORDER], sems, n, like)

    def over_xy(src, dst, sems, n, like):
        return send_all([(src, dst, device(dx, dy, 0, 0)) for dx, dy in XYORDER], sems, n, like)

    def stage0(n):
        zfirst, off, width = CHUNKS[n]
        cols = pl.ds(off, width)
        if zfirst:
            start = 2 * PLANE + off
            terms(start, width)
            pieces = [(term.at[out_rows[d], pl.ds(start, width)], rc1.at[d, :, cols], device(0, 0, d, 0)) for d in ZORDER]
            return send_all(pieces, sem1, n, rc1.at[1:NZ, :, cols])
        for side in range(2):
            terms(side * PLANE + off, width)
        pieces = []
        for dx, dy in XYORDER:
            rows, col = out_plane[dx, dy]
            src = term.at[rows, pl.ds(hint(col + off, 128), width)]
            pieces.append((src, ra1.at[dx * NY + dy, :, cols], device(dx, dy, 0, 0)))
        return send_all(pieces, sem1, n, ra1.at[1 : NX * NY, :, cols])

    def stage1(n):
        zfirst, off, width = CHUNKS[n]
        cols = pl.ds(off, width)
        first[n].wait_recv()
        if zfirst:
            value = term[z_rows, pl.ds(2 * PLANE + off, width)]
            for d in range(1, NZ):
                value = value + rc1[d, :, cols]
            rc2[plane, :, cols] = value
            piece = rc2.at[plane, :, cols]
            return over_xy(piece, piece, sem2, n, rc2.at[1 : NX * NY, :, cols])
        value = term[plane_rows, pl.ds(hint(plane_col + off, 128), width)]
        for d in range(1, NX * NY):
            value = value + ra1[d, :, cols]
        ra2[z, :, cols] = value
        piece = ra2.at[z, :, cols]
        return over_z(piece, piece, sem2, n, ra2.at[1:NZ, :, cols])

    def stage2(n):
        zfirst, off, width = CHUNKS[n]
        cols = pl.ds(off, width)
        second[n].wait_recv()
        if zfirst:
            value = rc2[0, :, cols]
            for k in range(1, NX * NY):
                value = value + rc2[k, :, cols]
            place = (z_rows, pl.ds(hint(c * HALF + 2 * PLANE + off, 128), width))
            total[place] = value
            return over_z(total.at[place], total.at[place], sem3, n, rc1.at[1:NZ, :, cols])
        value = ra2[0, :, cols]
        for k in range(1, NZ):
            value = value + ra2[k, :, cols]
        place = (plane_rows, pl.ds(hint(c * HALF + plane_col + off, 128), width))
        total[place] = value
        return over_xy(total.at[place], total.at[place], sem3, n, ra1.at[1 : NX * NY, :, cols])

    def ranges(n, core):
        zfirst, off, width = CHUNKS[n]
        starts = (2 * PLANE + off,) if zfirst else (off, PLANE + off)
        return [pl.ds(hint(core * HALF + start, 128), width) for start in starts]

    def stage3(n):
        third[n].wait_recv()
        places = [total.at[:, cols] for cols in ranges(n, c)]
        return send_all([(p, p, sibling) for p in places], fwd_sem, n, term.at[:, 0 : len(places) * CHUNKS[n][2]])

    share = x * 2 + c

    def gram_start():
        gfull[...] = dot(jnp.transpose(left)[:RANK], left)
        gy[y] = gfull[pl.ds(hint(share * 8, 8), 8), :]
        pieces = [(gy.at[y], gy.at[y], device(0, d, 0, 0)) for d in (2, 1, 3)]
        return send_all(pieces, gram_sem, 0, gy.at[1:NY])

    def gram_middle(copies):
        copies.wait_recv()
        gz[z] = ((gy[0] + gy[1]) + gy[2]) + gy[3]
        return over_z(gz.at[z], gz.at[z], gram_sem, 1, gz.at[1:NZ])

    def gram_end(copies):
        copies.wait_recv()
        value = gz[0]
        for k in range(1, NZ):
            value = value + gz[k]
        gx[share] = value
        pieces = [(gx.at[share], gx.at[share], device(dx, 0, 0, dc)) for dx, dc in PLANEORDER]
        return send_all(pieces, gram_sem, 2, gx.at[1:8])

    def gram_blocks():
        lane = lax.broadcasted_iota(jnp.int32, (8, 2 * RANK), 1)
        row = lax.broadcasted_iota(jnp.int32, (8, 2 * RANK), 0)
        return [
            jnp.where(lane < RANK, gx[k], jnp.where(lane == row + (RANK + 8 * k), 1.0, 0.0)) for k in range(RANK // 8)
        ]

    def coefficients(blocks):
        whole = jnp.concatenate(blocks, axis=0)
        lane = lax.broadcasted_iota(jnp.int32, (RANK, 2 * RANK), 1)
        row = lax.broadcasted_iota(jnp.int32, (RANK, 2 * RANK), 0)
        pivot = jnp.sum(jnp.where(lane == row, whole, 0.0), axis=1, keepdims=True)
        scale = lax.rsqrt(pivot)
        scale = scale * (1.5 - 0.5 * pivot * scale * scale)
        inverse = (pltpu.roll(whole, RANK, 1) * scale)[:, :RANK]
        own = l96[pl.ds(hint(c * ROWS, 8), ROWS), 0:RANK]
        ortho = dot_nt(own, inverse)
        both = 0.25 * jnp.concatenate([inverse, dot(ortho, inverse)], axis=0)
        high, low = split(both)
        coef[...] = jnp.concatenate([high, high, low, low], axis=1)

    def update(cols):
        high, low = split(total[:, cols])
        both = bdot(coef[...], jnp.concatenate([high, low, high, low], axis=0))
        new_basis[:, cols] = both[:RANK]
        approx = both[RANK:]
        new_error[:, cols] = merged[:, cols] - approx
        speed = nesterov_mu * m_buf[:, cols] + approx
        new_momentum[:, cols] = speed
        stepped = w_buf[:, cols] - outer_rate * (approx + nesterov_mu * speed)
        new_weights[:, cols] = stepped
        new_anchor[:, cols] = anchor_decay * a_buf[:, cols] + (1.0 - anchor_decay) * stepped

    def update_own(n):
        for cols in ranges(n, c):
            update(cols)

    def update_sibling(n):
        fourth[n].wait_recv()
        for cols in ranges(n, 1 - c):
            update(cols)

    early = count // 2
    gram = gram_start()
    first = [stage0(n) for n in range(count)]
    gram = gram_middle(gram)
    second = [stage1(n) for n in range(count)]
    gram = gram_end(gram)
    third = [stage2(n) for n in range(count)]
    gram.wait_recv()
    coefficients(eliminate(gram_blocks(), 0, RANK))
    for copy in late:
        copy.wait()
    fourth = []
    for n in range(count):
        fourth.append(stage3(n))
        if n:
            update_own(n - 1)
    for n in range(count - 1):
        update_sibling(n)
    update_own(count - 1)
    update_sibling(count - 1)
    for copy in pending:
        copy.wait_send()


def store_kernel(*refs):
    sems = refs[-1]
    count = len(refs) // 2
    copies = [pltpu.make_async_copy(refs[k], refs[count + k], sems.at[k]) for k in range(count)]
    for copy in copies:
        copy.start()
    for copy in copies:
        copy.wait()


def per_device(delta, error, weights, momentum, anchor, basis):
    count = len(CHUNKS)
    hbm = pl.BlockSpec(memory_space=pltpu.HBM)
    vmem = pl.BlockSpec(memory_space=pltpu.VMEM)
    dma = pltpu.SemaphoreType.DMA
    shapes = [jax.ShapeDtypeStruct((ROWS, D), F32)] * 4 + [jax.ShapeDtypeStruct((RANK, D), F32)]
    outs = pl.pallas_call(
        step_kernel,
        out_shape=shapes,
        in_specs=[hbm] * 6,
        out_specs=[vmem] * 5,
        scratch_shapes=[
            pltpu.VMEM((ROWS, D), F32),
            pltpu.VMEM((ROWS, D), F32),
            pltpu.VMEM((RANK, D), F32),
            pltpu.VMEM((ROWS, D), F32),
            pltpu.VMEM((ROWS, D), F32),
            pltpu.VMEM((ROWS, D), F32),
            pltpu.VMEM((ROWS, D), F32),
            pltpu.VMEM((RANK, D), F32),
            pltpu.VMEM((RANK + ROWS, 4 * RANK), BF16),
            pltpu.VMEM((ROWS, HALF), F32),
            pltpu.VMEM((4 * ROWS, HALF), BF16),
            pltpu.VMEM((2 * NX, ROWS // 2, 2 * RANK), F32),
            pltpu.VMEM((2 * ROWS, 2 * RANK), F32),
            pltpu.VMEM((RANK, HALF), F32),
            pltpu.VMEM((NX * NY, 8, PLANE), F32),
            pltpu.VMEM((NZ, 8, ZFIRST), F32),
            pltpu.VMEM((NZ, 8, PLANE), F32),
            pltpu.VMEM((NX * NY, 8, ZFIRST), F32),
            pltpu.VMEM((RANK, 2 * RANK), F32),
            pltpu.VMEM((NY, 8, 2 * RANK), F32),
            pltpu.VMEM((NZ, 8, 2 * RANK), F32),
            pltpu.VMEM((8, 8, 2 * RANK), F32),
            dma((D // LOAD, 3)),
            dma((3,)),
            dma((2, 1)),
            dma((2, 1)),
            dma((2, count)),
            dma((2, count)),
            dma((2, count)),
            dma((2, count)),
            dma((2, 3)),
        ],
        compiler_params=pltpu.CompilerParams(collective_id=0, has_side_effects=True, vmem_limit_bytes=32 << 20),
    )(*(pltpu.with_memory_space_constraint(a, pltpu.HBM) for a in (delta[0], error[0], basis.T, weights, momentum, anchor)))
    outs = pl.pallas_call(
        store_kernel,
        out_shape=shapes,
        in_specs=[vmem] * 5,
        out_specs=[hbm] * 5,
        scratch_shapes=[dma((5,))],
        compiler_params=pltpu.CompilerParams(vmem_limit_bytes=1 << 20),
    )(*(pltpu.with_memory_space_constraint(a, pltpu.VMEM) for a in outs))
    new_weights, new_momentum, new_anchor, new_error, new_basis = outs
    return (new_weights, new_momentum, new_anchor, new_error[None], new_basis.T)


def solution(mesh):
    in_specs = (
        P("group", "shard", None),
        P("group", "shard", None),
        P("shard", None),
        P("shard", None),
        P("shard", None),
        P(),
    )
    out_specs = (
        P("shard", None),
        P("shard", None),
        P("shard", None),
        P("group", "shard", None),
        P(),
    )
    return jax.shard_map(
        per_device, mesh=mesh, in_specs=in_specs, out_specs=out_specs, check_vma=False
    )
```

```python
import jax
import jax.numpy as jnp
from jax import lax
from jax.experimental import pallas as pl
from jax.experimental.pallas import tpu as pltpu
from jax.sharding import PartitionSpec as P

MESH = pl.DeviceIdType.MESH
HIGHEST = lax.Precision.HIGHEST
F32 = jnp.float32
BF16 = jnp.bfloat16

outer_rate = 0.7
nesterov_mu = 0.9
anchor_decay = 0.9

D = 5120
RANK = 64
ROWS = 48
NX, NY, NZ = 4, 4, 8
HALF = D // 2
PLANE = 896
ZFIRST = HALF - 2 * PLANE
CHUNKS = ((True, 0, 256), (False, 0, 256), (True, 256, 256), (False, 256, 256), (True, 512, 256), (False, 512, 256), (False, 768, 128))
LOAD = 1280
GROUP = 4
ZORDER = (4, 3, 5, 2, 6, 1, 7)
PLANEORDER = ((2, 0), (2, 1), (1, 0), (3, 0), (1, 1), (3, 1), (0, 1))
XYORDER = ((2, 2), (2, 1), (2, 3), (1, 2), (3, 2), (2, 0), (0, 2), (1, 1), (1, 3), (3, 1), (3, 3), (1, 0), (3, 0), (0, 1), (0, 3))


def hint(value, multiple):
    return pl.multiple_of(value, multiple)


def dot_nt(a, b):
    return lax.dot_general(a, b, (((1,), (1,)), ((), ())), precision=HIGHEST, preferred_element_type=F32)


def dot(a, b):
    return jnp.dot(a, b, precision=HIGHEST, preferred_element_type=F32)


def split(value):
    high = value.astype(BF16)
    return high, (value - high.astype(F32)).astype(BF16)


def bdot(a, b):
    return jnp.dot(a, b, preferred_element_type=F32)


def eliminate(blocks, first, last):
    index = lax.broadcasted_iota(jnp.int32, (8, 1), 0)
    for j in range(first, last, GROUP):
        own, at = j // 8, j % 8
        steps = range(GROUP)
        columns = {
            (k, t): jnp.broadcast_to(blocks[k][:, j + t : j + t + 1], (8, 2 * RANK))
            for k in range(own, RANK // 8) for t in steps
        }
        rows = [blocks[own][at + t : at + t + 1, :] for t in steps]
        small = {(i, t): columns[own, t][at + i : at + i + 1, :] for i in steps for t in steps}
        unit, ratio = [], {}
        for t in steps:
            inverse = 1.0 / small[t, t]
            unit.append(rows[t] * inverse)
            for i in range(t + 1, GROUP):
                ratio[t, i] = small[t, i] * inverse
            for i in range(t + 1, GROUP):
                rows[i] = rows[i] - small[i, t] * unit[t]
                for k in range(t + 1, GROUP):
                    small[i, k] = small[i, k] - small[i, t] * ratio[t, k]
        for k in range(own, RANK // 8):
            value, done = blocks[k], []
            for t in steps:
                column = columns[k, t]
                for i in range(t):
                    column = column - done[i] * ratio[i, t]
                done.append(column)
                value = value - column * unit[t]
            if k == own:
                value = jnp.where(index >= at + GROUP, value, blocks[k])
                for t in steps:
                    value = jnp.where(index == at + t, rows[t], value)
            blocks[k] = value
    return blocks


def step_kernel(
    delta, error, basis_t, weights, momentum, anchor,
    new_weights, new_momentum, new_anchor, new_error, new_basis,
    d_buf, e_buf, b_buf, w_buf, m_buf, a_buf, merged, total, coef, msib, mst, lbuf, l96, term, ra1, rc1, ra2, rc2, gfull, gy, gz, gx,
    load_sem, late_sem, sib_sem, left_sem, sem1, sem2, sem3, fwd_sem, gram_sem,
):
    x = lax.axis_index("group")
    shard = lax.axis_index("shard")
    z = lax.div(shard, 8)
    y = lax.rem(lax.div(shard, 2), 4)
    c = lax.rem(shard, 2)
    plane = x * NY + y

    xs = [lax.rem(x + d, NX) for d in range(NX)]
    ys = [lax.rem(y + d, NY) for d in range(NY)]
    zs = [lax.rem(z + d, NZ) for d in range(NZ)]
    cs = [c, 1 - c]
    known = {}

    def device(dx, dy, dz, dc):
        key = (dx, dy, dz, dc)
        if key not in known:
            known[key] = (xs[dx], zs[dz] * 8 + ys[dy] * 2 + cs[dc])
        return known[key]

    sibling = device(0, 0, 0, 1)

    barrier = pltpu.get_barrier_semaphore()
    peers = [device(0, 0, d, 0) for d in ZORDER]
    peers += [device(dx, dy, 0, 0) for dx, dy in XYORDER]
    peers += [device(dx, 0, 0, 1) for dx in (2, 1, 3, 0)]
    for peer in peers:
        pl.semaphore_signal(barrier, inc=1, device_id=peer, device_id_type=MESH)

    columns = [hint(((1 - c) * HALF + k * LOAD) % D, 128) for k in range(D // LOAD)]
    loads = []
    for k, col in enumerate(columns):
        cols = pl.ds(col, LOAD)
        group = []
        for j, (src, dst) in enumerate(((delta, d_buf), (error, e_buf), (basis_t, b_buf))):
            copy = pltpu.make_async_copy(src.at[:, cols], dst.at[:, cols], load_sem.at[k, j])
            copy.start()
            group.append(copy)
        loads.append(group)

    late = []
    for j, (src, dst) in enumerate(((weights, w_buf), (momentum, m_buf), (anchor, a_buf))):
        copy = pltpu.make_async_copy(src, dst, late_sem.at[j])
        copy.start()
        late.append(copy)

    pending = []

    def link(src, dst, sems, n, peer):
        return pltpu.make_async_remote_copy(
            src_ref=src, dst_ref=dst, send_sem=sems.at[0, n], recv_sem=sems.at[1, n],
            device_id=peer, device_id_type=MESH,
        )

    def send_all(pieces, sems, n, like):
        for src, dst, peer in pieces:
            link(src, dst, sems, n, peer).start()
        copy = link(like, like, sems, n, sibling)
        pending.append(copy)
        return copy

    mine = pl.ds(hint(c * ROWS, 16), ROWS)
    mine_low = pl.ds(hint((2 + c) * ROWS, 16), ROWS)
    theirs = pl.ds(hint((1 - c) * ROWS, 16), ROWS)
    theirs_low = pl.ds(hint((3 - c) * ROWS, 16), ROWS)
    part = jnp.zeros((2 * ROWS, 2 * RANK), F32)
    for k, col in enumerate(columns):
        for copy in loads[k]:
            copy.wait()
        cols = pl.ds(col, LOAD)
        value = d_buf[:, cols] + e_buf[:, cols]
        merged[:, cols] = value
        high, low = split(value)
        if k >= 2:
            mst[mine, (k - 2) * LOAD : (k - 1) * LOAD] = high
            mst[mine_low, (k - 2) * LOAD : (k - 1) * LOAD] = low
        part = part + lax.dot_general(
            jnp.concatenate([high, low], axis=0), jnp.concatenate(split(b_buf[:, cols]), axis=0),
            (((1,), (1,)), ((), ())), preferred_element_type=F32,
        )
    part = part[:ROWS] + part[ROWS:]
    part = part + pltpu.roll(part, RANK, 1)
    low_lanes = lax.broadcasted_iota(jnp.int32, (ROWS // 2, 2 * RANK), 1) < RANK
    lbuf[c * NX + x] = jnp.where(low_lanes, part[: ROWS // 2], part[ROWS // 2 :])

    pl.semaphore_wait(barrier, len(peers))
    slot = lbuf.at[c * NX + x]
    lefts = send_all([(slot, slot, device(dx, 0, 0, dc)) for dx, dc in PLANEORDER], left_sem, 0, lbuf.at[0:7])
    away = merged.at[:, pl.ds(hint((1 - c) * HALF, 128), HALF)]
    moved = send_all([(away, msib, sibling)], sib_sem, 0, msib)
    moved.wait_recv()
    mst[theirs, :], mst[theirs_low, :] = split(msib[...])
    lefts.wait_recv()
    for core in range(2):
        packed = ((lbuf[core * NX] + lbuf[core * NX + 1]) + lbuf[core * NX + 2]) + lbuf[core * NX + 3]
        l96[core * ROWS : core * ROWS + ROWS // 2, :] = jnp.where(low_lanes, packed, 0.0)
        l96[core * ROWS + ROWS // 2 : (core + 1) * ROWS, :] = jnp.where(low_lanes, pltpu.roll(packed, RANK, 1), 0.0)
    left = l96[...]
    left_high = left.astype(BF16).astype(F32)
    pair = left_high + pltpu.roll(left - left_high, RANK, 1)
    left_t = jnp.transpose(jnp.concatenate([pair, pair], axis=0)).astype(BF16)

    def terms(start, width):
        value = bdot(left_t, mst[:, start : start + width])
        term[:, start : start + width] = value[:RANK] + value[RANK:]

    count = len(CHUNKS)
    z_rows = pl.ds(hint(z * 8, 8), 8)
    plane_rows = pl.ds(hint(lax.div(plane, 2) * 8, 8), 8)
    plane_col = lax.rem(plane, 2) * PLANE
    out_rows = [pl.ds(hint(zs[d] * 8, 8), 8) for d in range(NZ)]
    out_plane = {}
    for dx, dy in XYORDER:
        piece = xs[dx] * NY + ys[dy]
        out_plane[dx, dy] = (pl.ds(hint(lax.div(piece, 2) * 8, 8), 8), lax.rem(piece, 2) * PLANE)

    def over_z(src, dst, sems, n, like):
        return send_all([(src, dst, device(0, 0, d, 0)) for d in ZORDER], sems, n, like)

    def over_xy(src, dst, sems, n, like):
        return send_all([(src, dst, device(dx, dy, 0, 0)) for dx, dy in XYORDER], sems, n, like)

    def stage0(n):
        zfirst, off, width = CHUNKS[n]
        cols = pl.ds(off, width)
        if zfirst:
            start = 2 * PLANE + off
            terms(start, width)
            pieces = [(term.at[out_rows[d], pl.ds(start, width)], rc1.at[d, :, cols], device(0, 0, d, 0)) for d in ZORDER]
            return send_all(pieces, sem1, n, rc1.at[1:NZ, :, cols])
        for side in range(2):
            terms(side * PLANE + off, width)
        pieces = []
        for dx, dy in XYORDER:
            rows, col = out_plane[dx, dy]
            src = term.at[rows, pl.ds(hint(col + off, 128), width)]
            pieces.append((src, ra1.at[dx * NY + dy, :, cols], device(dx, dy, 0, 0)))
        return send_all(pieces, sem1, n, ra1.at[1 : NX * NY, :, cols])

    def stage1(n):
        zfirst, off, width = CHUNKS[n]
        cols = pl.ds(off, width)
        first[n].wait_recv()
        if zfirst:
            value = term[z_rows, pl.ds(2 * PLANE + off, width)]
            for d in range(1, NZ):
                value = value + rc1[d, :, cols]
            rc2[plane, :, cols] = value
            piece = rc2.at[plane, :, cols]
            return over_xy(piece, piece, sem2, n, rc2.at[1 : NX * NY, :, cols])
        value = term[plane_rows, pl.ds(hint(plane_col + off, 128), width)]
        for d in range(1, NX * NY):
            value = value + ra1[d, :, cols]
        ra2[z, :, cols] = value
        piece = ra2.at[z, :, cols]
        return over_z(piece, piece, sem2, n, ra2.at[1:NZ, :, cols])

    def stage2(n):
        zfirst, off, width = CHUNKS[n]
        cols = pl.ds(off, width)
        second[n].wait_recv()
        if zfirst:
            value = rc2[0, :, cols]
            for k in range(1, NX * NY):
                value = value + rc2[k, :, cols]
            place = (z_rows, pl.ds(hint(c * HALF + 2 * PLANE + off, 128), width))
            total[place] = value
            return over_z(total.at[place], total.at[place], sem3, n, rc1.at[1:NZ, :, cols])
        value = ra2[0, :, cols]
        for k in range(1, NZ):
            value = value + ra2[k, :, cols]
        place = (plane_rows, pl.ds(hint(c * HALF + plane_col + off, 128), width))
        total[place] = value
        return over_xy(total.at[place], total.at[place], sem3, n, ra1.at[1 : NX * NY, :, cols])

    def ranges(n, core):
        zfirst, off, width = CHUNKS[n]
        starts = (2 * PLANE + off,) if zfirst else (off, PLANE + off)
        return [pl.ds(hint(core * HALF + start, 128), width) for start in starts]

    def stage3(n):
        third[n].wait_recv()
        places = [total.at[:, cols] for cols in ranges(n, c)]
        return send_all([(p, p, sibling) for p in places], fwd_sem, n, term.at[:, 0 : len(places) * CHUNKS[n][2]])

    share = x * 2 + c

    def gram_start():
        gfull[...] = dot(jnp.transpose(left)[:RANK], left)
        gy[y] = gfull[pl.ds(hint(share * 8, 8), 8), :]
        pieces = [(gy.at[y], gy.at[y], device(0, d, 0, 0)) for d in (2, 1, 3)]
        return send_all(pieces, gram_sem, 0, gy.at[1:NY])

    def gram_middle(copies):
        copies.wait_recv()
        gz[z] = ((gy[0] + gy[1]) + gy[2]) + gy[3]
        return over_z(gz.at[z], gz.at[z], gram_sem, 1, gz.at[1:NZ])

    def gram_end(copies):
        copies.wait_recv()
        value = gz[0]
        for k in range(1, NZ):
            value = value + gz[k]
        gx[share] = value
        pieces = [(gx.at[share], gx.at[share], device(dx, 0, 0, dc)) for dx, dc in PLANEORDER]
        return send_all(pieces, gram_sem, 2, gx.at[1:8])

    def gram_blocks():
        lane = lax.broadcasted_iota(jnp.int32, (8, 2 * RANK), 1)
        row = lax.broadcasted_iota(jnp.int32, (8, 2 * RANK), 0)
        return [
            jnp.where(lane < RANK, gx[k], jnp.where(lane == row + (RANK + 8 * k), 1.0, 0.0)) for k in range(RANK // 8)
        ]

    def coefficients(blocks):
        whole = jnp.concatenate(blocks, axis=0)
        lane = lax.broadcasted_iota(jnp.int32, (RANK, 2 * RANK), 1)
        row = lax.broadcasted_iota(jnp.int32, (RANK, 2 * RANK), 0)
        pivot = jnp.sum(jnp.where(lane == row, whole, 0.0), axis=1, keepdims=True)
        scale = lax.rsqrt(pivot)
        scale = scale * (1.5 - 0.5 * pivot * scale * scale)
        inverse = (pltpu.roll(whole, RANK, 1) * scale)[:, :RANK]
        own = l96[pl.ds(hint(c * ROWS, 8), ROWS), 0:RANK]
        ortho = dot_nt(own, inverse)
        both = 0.25 * jnp.concatenate([inverse, dot(ortho, inverse)], axis=0)
        high, low = split(both)
        coef[...] = jnp.concatenate([high, high, low, low], axis=1)

    def update(cols):
        high, low = split(total[:, cols])
        both = bdot(coef[...], jnp.concatenate([high, low, high, low], axis=0))
        new_basis[:, cols] = both[:RANK]
        approx = both[RANK:]
        new_error[:, cols] = merged[:, cols] - approx
        speed = nesterov_mu * m_buf[:, cols] + approx
        new_momentum[:, cols] = speed
        stepped = w_buf[:, cols] - outer_rate * (approx + nesterov_mu * speed)
        new_weights[:, cols] = stepped
        new_anchor[:, cols] = anchor_decay * a_buf[:, cols] + (1.0 - anchor_decay) * stepped

    def update_own(n):
        for cols in ranges(n, c):
            update(cols)

    def update_sibling(n):
        fourth[n].wait_recv()
        for cols in ranges(n, 1 - c):
            update(cols)

    early = count // 2
    first = [stage0(0)]
    gram = gram_start()
    first += [stage0(n) for n in range(1, count)]
    gram = gram_middle(gram)
    second = [stage1(n) for n in range(count)]
    gram = gram_end(gram)
    third = [stage2(n) for n in range(count)]
    gram.wait_recv()
    coefficients(eliminate(gram_blocks(), 0, RANK))
    for copy in late:
        copy.wait()
    fourth = []
    for n in range(count):
        fourth.append(stage3(n))
        if n:
            update_own(n - 1)
    for n in range(count - 1):
        update_sibling(n)
    update_own(count - 1)
    update_sibling(count - 1)
    for copy in pending:
        copy.wait_send()


def store_kernel(*refs):
    sems = refs[-1]
    count = len(refs) // 2
    copies = [pltpu.make_async_copy(refs[k], refs[count + k], sems.at[k]) for k in range(count)]
    for copy in copies:
        copy.start()
    for copy in copies:
        copy.wait()


def per_device(delta, error, weights, momentum, anchor, basis):
    count = len(CHUNKS)
    hbm = pl.BlockSpec(memory_space=pltpu.HBM)
    vmem = pl.BlockSpec(memory_space=pltpu.VMEM)
    dma = pltpu.SemaphoreType.DMA
    shapes = [jax.ShapeDtypeStruct((ROWS, D), F32)] * 4 + [jax.ShapeDtypeStruct((RANK, D), F32)]
    outs = pl.pallas_call(
        step_kernel,
        out_shape=shapes,
        in_specs=[hbm] * 6,
        out_specs=[vmem] * 5,
        scratch_shapes=[
            pltpu.VMEM((ROWS, D), F32),
            pltpu.VMEM((ROWS, D), F32),
            pltpu.VMEM((RANK, D), F32),
            pltpu.VMEM((ROWS, D), F32),
            pltpu.VMEM((ROWS, D), F32),
            pltpu.VMEM((ROWS, D), F32),
            pltpu.VMEM((ROWS, D), F32),
            pltpu.VMEM((RANK, D), F32),
            pltpu.VMEM((RANK + ROWS, 4 * RANK), BF16),
            pltpu.VMEM((ROWS, HALF), F32),
            pltpu.VMEM((4 * ROWS, HALF), BF16),
            pltpu.VMEM((2 * NX, ROWS // 2, 2 * RANK), F32),
            pltpu.VMEM((2 * ROWS, 2 * RANK), F32),
            pltpu.VMEM((RANK, HALF), F32),
            pltpu.VMEM((NX * NY, 8, PLANE), F32),
            pltpu.VMEM((NZ, 8, ZFIRST), F32),
            pltpu.VMEM((NZ, 8, PLANE), F32),
            pltpu.VMEM((NX * NY, 8, ZFIRST), F32),
            pltpu.VMEM((RANK, 2 * RANK), F32),
            pltpu.VMEM((NY, 8, 2 * RANK), F32),
            pltpu.VMEM((NZ, 8, 2 * RANK), F32),
            pltpu.VMEM((8, 8, 2 * RANK), F32),
            dma((D // LOAD, 3)),
            dma((3,)),
            dma((2, 1)),
            dma((2, 1)),
            dma((2, count)),
            dma((2, count)),
            dma((2, count)),
            dma((2, count)),
            dma((2, 3)),
        ],
        compiler_params=pltpu.CompilerParams(collective_id=0, has_side_effects=True, vmem_limit_bytes=32 << 20),
    )(*(pltpu.with_memory_space_constraint(a, pltpu.HBM) for a in (delta[0], error[0], basis.T, weights, momentum, anchor)))
    outs = pl.pallas_call(
        store_kernel,
        out_shape=shapes,
        in_specs=[vmem] * 5,
        out_specs=[hbm] * 5,
        scratch_shapes=[dma((5,))],
        compiler_params=pltpu.CompilerParams(vmem_limit_bytes=1 << 20),
    )(*(pltpu.with_memory_space_constraint(a, pltpu.VMEM) for a in outs))
    new_weights, new_momentum, new_anchor, new_error, new_basis = outs
    return (new_weights, new_momentum, new_anchor, new_error[None], new_basis.T)


def solution(mesh):
    in_specs = (
        P("group", "shard", None),
        P("group", "shard", None),
        P("shard", None),
        P("shard", None),
        P("shard", None),
        P(),
    )
    out_specs = (
        P("shard", None),
        P("shard", None),
        P("shard", None),
        P("group", "shard", None),
        P(),
    )
    return jax.shard_map(
        per_device, mesh=mesh, in_specs=in_specs, out_specs=out_specs, check_vma=False
    )
```
